128 devices in a mesh: row: 4 (over x_lo, core), col: 32 (over z, x_hi, y).
Axes of the slice: x: 4 (x_hi: 2, x_lo: 2; x = x_hi * 2 + x_lo), y: 4, z: 4, core: 2. Of those that a mesh axis runs over, the one named last changes fastest.
Arguments:
- images: bfloat16 [16384, 1280], P(('row', 'col')), may hold values from -0.5 to 0.5
- texts: bfloat16 [16384, 1280], P(('col', 'row')), may hold values from -0.5 to 0.5
- logit_scale: float32 [], replicated, may hold values from 30 to 100
Outputs:
- loss: float32 [], replicated
- grad_images: float32 [16384, 1280], P(('row', 'col'))
- grad_texts: float32 [16384, 1280], P(('col', 'row'))
- grad_scale: float32 [], replicated
The draws below stay inside these ranges and needn't reach their ends.
All inputs are finite; a program needn't handle non-finite values.
Results may differ from the reference program's by a relative error of at most 0.0024.
Values may be sent and summed in bfloat16 or wider, within the bound.
No kernel may reach another device: no remote copies, remote signals or barrier semaphores. Data moves between devices by JAX's collectives and lax.ppermute only.
A program may use at most 128 MiB of HBM per device.

```python
import math
import jax
import jax.numpy as jnp
from jax import lax

E = 1280
TOKENS = 16384


def pair_base(key):
    keys = jax.random.split(key, 4)
    root = math.sqrt(E)
    shared = jnp.clip(jax.random.normal(keys[0], (TOKENS, E), jnp.float32), -4.0, 4.0) / root
    private = jnp.clip(jax.random.normal(keys[1], (TOKENS, E), jnp.float32), -4.0, 4.0) / root
    order = jnp.arange(TOKENS, dtype=jnp.float32)[:, None] / TOKENS
    rising = jnp.power(3.0, order)
    image_scale = 0.1 * jnp.power(10.0, jax.random.uniform(keys[2], (TOKENS, 1), jnp.float32)) * rising
    text_scale = 0.1 * jnp.power(10.0, jax.random.uniform(keys[3], (TOKENS, 1), jnp.float32)) * rising
    return (shared, private, image_scale, text_scale)


def draw_images(key, part):
    shared, private, image_scale, text_scale = pair_base(key)
    images = (0.3 * shared + 0.95 * private) * image_scale
    return jnp.clip(images, -0.5, 0.5).astype(jnp.bfloat16)


def draw_texts(key, part):
    shared, private, image_scale, text_scale = pair_base(key)
    texts = shared * text_scale
    return jnp.clip(texts, -0.5, 0.5).astype(jnp.bfloat16)


def setup_inputs(seed: int = 0) -> dict:
    streams_of = jax.random.split(jax.random.key(seed), 4)
    return {
        "images": draw_images(jax.random.fold_in(streams_of[3], 71), 0),
        "texts": draw_texts(jax.random.fold_in(streams_of[3], 71), 0),
        "logit_scale": jnp.clip(jnp.exp(jax.random.uniform(streams_of[2], (), jnp.float32, math.log(30.0), math.log(100.0))), 30.0, 100.0),
    }


def reference(images, texts, logit_scale):
    pair_total = images.shape[0]
    features = images.shape[1]
    step_rows = min(1024, pair_total)
    block_count = pair_total // step_rows
    image_blocks = images.reshape(block_count, step_rows, features)
    offsets = jnp.arange(block_count, dtype=jnp.int32) * step_rows
    text_ids = jnp.arange(pair_total, dtype=jnp.int32)

    def make_scores(image_rows):
        return logit_scale * lax.dot_general(image_rows, texts, (((1,), (1,)), ((), ())), preferred_element_type=jnp.float32)

    def forward(carry, inputs):
        col_max, col_sum = carry
        image_rows, offset = inputs
        scores = make_scores(image_rows)
        row_max = jnp.max(scores, axis=1)
        row_lse = row_max + jnp.log(jnp.sum(jnp.exp(scores - row_max[:, None]), axis=1))
        block_max = jnp.max(scores, axis=0)
        new_max = jnp.maximum(col_max, block_max)
        new_sum = col_sum * jnp.exp(col_max - new_max) + jnp.sum(jnp.exp(scores - new_max[None, :]), axis=0)
        image_ids = offset + jnp.arange(step_rows, dtype=jnp.int32)
        matched = image_ids[:, None] == text_ids[None, :]
        diagonal = jnp.sum(jnp.where(matched, scores, 0.0))
        return (new_max, new_sum), (row_lse, diagonal)

    start_state = (jnp.full((pair_total,), -jnp.inf, jnp.float32), jnp.zeros((pair_total,), jnp.float32))
    (col_max, col_sum), (row_lse, diagonal) = lax.scan(forward, start_state, (image_blocks, offsets))
    col_lse = col_max + jnp.log(col_sum)
    loss = (jnp.sum(row_lse) + jnp.sum(col_lse) - 2.0 * jnp.sum(diagonal)) / (2.0 * pair_total)

    def backward(carry, inputs):
        text_accum, scale_accum = carry
        image_rows, offset, block_lse = inputs
        scores = make_scores(image_rows)
        image_ids = offset + jnp.arange(step_rows, dtype=jnp.int32)
        matched = image_ids[:, None] == text_ids[None, :]
        weights = (jnp.exp(scores - block_lse[:, None]) + jnp.exp(scores - col_lse[None, :])) / (2.0 * pair_total)
        weights = weights - jnp.where(matched, 1.0 / pair_total, 0.0)
        scale_accum = scale_accum + jnp.sum(weights * scores)
        rounded = weights.astype(jnp.bfloat16)
        image_grad = logit_scale * jnp.dot(rounded, texts, preferred_element_type=jnp.float32)
        text_accum = text_accum + logit_scale * lax.dot_general(rounded, image_rows, (((0,), (0,)), ((), ())), preferred_element_type=jnp.float32)
        return (text_accum, scale_accum), image_grad

    back_state = (jnp.zeros((pair_total, features), jnp.float32), jnp.zeros((), jnp.float32))
    (grad_texts, scale_sum), image_grads = lax.scan(backward, back_state, (image_blocks, offsets, row_lse))
    grad_images = image_grads.reshape(pair_total, features)
    return loss, grad_images, grad_texts, scale_sum / logit_scale
```

```python
import functools
import itertools

import jax
import jax.numpy as jnp
import numpy as np
from jax import lax
from jax.experimental import pallas as pl
from jax.experimental.pallas import tpu as pltpu
from jax.sharding import PartitionSpec as P

LOG2E = 1.4426950408889634
LN2 = 0.6931471805599453
AXES = ("row", "col")
ROWS = 256


def linear(x, y, z, core):
    return (((x % 2) * 2 + core) * 4 + z) * 8 + (x // 2) * 4 + y


def devices():
    return itertools.product(range(4), range(4), range(4), range(2))


def partner_perm():
    return [(linear(x, y, z, c), linear(x, y, z, 1 - c)) for x, y, z, c in devices()]


def group_of(x, y, z, core):
    if core == 0:
        return sorted(linear(a, b, z, 0) for a in (x, 3 - x) for b in range(4))
    return sorted(linear(a, y, b, 1) for a in (x, x ^ 1) for b in range(4))


def groups():
    return sorted(set(tuple(group_of(*d)) for d in devices()))


def block_ids(x, y, z, core):
    out = []
    for member in group_of(x, y, z, core):
        row, col = member // 32, member % 32
        for c in (0, 1):
            at = (row // 2) * 2 + c
            out.append(at * 32 + col if core == 0 else col * 4 + at)
    return out


def match_table():
    table = np.full((128, 16), -1, np.int32)
    for x, y, z, c in devices():
        own, other = block_ids(x, y, z, c), block_ids(x, y, z, 1 - c)
        for k, block in enumerate(own):
            if block in other:
                table[linear(x, y, z, c), k] = other.index(block)
    return table


def to_column(row):
    n = row.shape[1]
    eye = lax.broadcasted_iota(jnp.int32, (n, n), 0) == lax.broadcasted_iota(jnp.int32, (n, n), 1)
    return jnp.sum(jnp.where(eye, jnp.broadcast_to(row, (n, n)), 0.0), axis=1, keepdims=True)


def to_row(column):
    n = column.shape[0]
    eye = lax.broadcasted_iota(jnp.int32, (n, n), 0) == lax.broadcasted_iota(jnp.int32, (n, n), 1)
    return jnp.sum(jnp.where(eye, jnp.broadcast_to(column, (n, n)), 0.0), axis=0, keepdims=True)


def score_kernel(scale_ref, own_ref, other_ref, scores_ref, stats_ref):
    scores = scale_ref[0] * lax.dot_general(
        own_ref[...], other_ref[...], (((1,), (1,)), ((), ())), preferred_element_type=jnp.float32
    )
    scores_ref[...] = scores
    peak = jnp.max(scores, axis=1, keepdims=True)
    total = jnp.sum(jnp.exp2(scores - peak), axis=1, keepdims=True)
    stats_ref[0:1, :] = to_row(peak)
    stats_ref[1:2, :] = to_row(total)


def score_call(scale, own, other):
    n, width = own.shape
    m = other.shape[0]
    return pl.pallas_call(
        score_kernel,
        grid=(n // ROWS,),
        in_specs=[
            pl.BlockSpec(memory_space=pltpu.SMEM),
            pl.BlockSpec((ROWS, width), lambda i: (i, 0)),
            pl.BlockSpec((m, width), lambda i: (0, 0)),
        ],
        out_specs=[
            pl.BlockSpec((ROWS, m), lambda i: (i, 0)),
            pl.BlockSpec((2, ROWS), lambda i: (0, i)),
        ],
        out_shape=[
            jax.ShapeDtypeStruct((n, m), jnp.float32),
            jax.ShapeDtypeStruct((2, n), jnp.float32),
        ],
        compiler_params=pltpu.CompilerParams(vmem_limit_bytes=48 * 1024 * 1024),
        cost_estimate=pl.CostEstimate(
            flops=2 * n * m * width, bytes_accessed=4 * n * m, transcendentals=n * m
        ),
        name="scores",
    )(scale, own, other)


def grad_kernel(
    pairs, match_ref, scale_ref, scores_ref, own_lse_ref, other_lse_ref, other_ref, grad_ref, sums_ref, weights
):
    step = pl.program_id(0)
    own_lse = to_column(own_lse_ref[...])
    scores = scores_ref[...]
    weight = jnp.exp2(scores - own_lse) + jnp.exp2(scores - other_lse_ref[...])
    weights[...] = weight.astype(jnp.bfloat16)
    partial = jnp.sum(weight * scores, axis=0, keepdims=True)
    dots = functools.reduce(
        jnp.add, [partial[:, k * 128 : (k + 1) * 128] for k in range(partial.shape[1] // 128)]
    )

    @pl.when(step == 0)
    def _():
        sums_ref[...] = jnp.zeros_like(sums_ref)

    sums_ref[0:1, :] += dots
    for half in range(ROWS // 128):
        place = match_ref[step * (ROWS // 128) + half]

        @pl.when(place >= 0)
        def _():
            rows = pl.ds(half * 128, 128)
            columns = pl.ds(pl.multiple_of(place * 128, 128), 128)
            corner = scores_ref[rows, columns]
            eye = lax.broadcasted_iota(jnp.int32, (128, 128), 0) == lax.broadcasted_iota(
                jnp.int32, (128, 128), 1
            )
            fixed = jnp.exp2(corner - own_lse[half * 128 : (half + 1) * 128]) + jnp.exp2(
                corner - other_lse_ref[:, columns]
            )
            weights[rows, columns] = (fixed - jnp.where(eye, 1.0 / pairs, 0.0)).astype(jnp.bfloat16)
            sums_ref[1:2, :] += jnp.sum(jnp.where(eye, corner, 0.0), axis=0, keepdims=True)

    grad_ref[...] = (
        scale_ref[0] * jnp.dot(weights[...], other_ref[...], preferred_element_type=jnp.float32)
    ).astype(grad_ref.dtype)


def grad_call(pairs, match, scale, scores, own_lse, other_lse, other):
    n, m = scores.shape
    width = other.shape[1]
    return pl.pallas_call(
        functools.partial(grad_kernel, pairs),
        grid=(n // ROWS,),
        in_specs=[
            pl.BlockSpec(memory_space=pltpu.SMEM),
            pl.BlockSpec(memory_space=pltpu.SMEM),
            pl.BlockSpec((ROWS, m), lambda i: (i, 0)),
            pl.BlockSpec((1, ROWS), lambda i: (0, i)),
            pl.BlockSpec((1, m), lambda i: (0, 0)),
            pl.BlockSpec((m, width), lambda i: (0, 0)),
        ],
        out_specs=[
            pl.BlockSpec((ROWS, width), lambda i: (i, 0)),
            pl.BlockSpec((2, 128), lambda i: (0, 0)),
        ],
        out_shape=[
            jax.ShapeDtypeStruct((n, width), jnp.bfloat16),
            jax.ShapeDtypeStruct((2, 128), jnp.float32),
        ],
        scratch_shapes=[pltpu.VMEM((ROWS, m), jnp.bfloat16)],
        compiler_params=pltpu.CompilerParams(vmem_limit_bytes=48 * 1024 * 1024),
        cost_estimate=pl.CostEstimate(
            flops=2 * n * m * width, bytes_accessed=4 * n * m, transcendentals=2 * n * m
        ),
        name="grads",
    )(match, scale, scores, own_lse, other_lse, other)


def on_device(images, texts, logit_scale):
    shard, width = images.shape
    pairs = shard * 128
    me = lax.axis_index(AXES)
    first = lax.rem(lax.axis_index("row"), 2) == 0
    swap = functools.partial(lax.ppermute, axis_name=AXES, perm=partner_perm())
    members = [list(g) for g in groups()]

    def spread(value):
        everywhere = jnp.broadcast_to(value[None], (8,) + value.shape)
        return lax.all_to_all(everywhere, AXES, 0, 0, axis_index_groups=members, tiled=True)

    got = swap(jnp.where(first, texts, images))
    mine = jnp.where(first, images, texts)
    chip = jnp.concatenate([jnp.where(first, mine, got), jnp.where(first, got, mine)], axis=0)
    own = spread(chip).reshape(16 * shard, width)
    other = swap(own)

    scale2 = (logit_scale * LOG2E).reshape(1)
    scores, stats = score_call(scale2, own, other)
    all_stats = spread(stats)
    peak = jnp.max(all_stats[:, 0], axis=0, keepdims=True)
    total = jnp.sum(all_stats[:, 1] * jnp.exp2(all_stats[:, 0] - peak), axis=0, keepdims=True)
    own_lse = peak + jnp.log2(total)
    other_lse = swap(own_lse)

    shift = float(np.log2(2.0 * pairs))
    match = lax.dynamic_slice(jnp.asarray(match_table()), (me, 0), (1, 16)).reshape(16)
    grads, sums = grad_call(
        pairs, match, logit_scale.reshape(1), scores, own_lse + shift, other_lse + shift, other
    )
    diagonal = jnp.sum(sums[1]) * LN2
    weighted = jnp.sum(sums[0]) * LN2
    loss_part = jnp.sum(own_lse) * (LN2 / 8.0) - diagonal
    scale_part = 0.5 * (weighted - diagonal / pairs) / logit_scale
    parts = jnp.broadcast_to(jnp.stack([loss_part, scale_part])[:, None], (2, 128))

    received = lax.all_to_all(
        grads.reshape(8, 2 * shard, width), AXES, 0, 0, axis_index_groups=members, tiled=True
    )
    summed = jnp.sum(received.astype(jnp.float32), axis=0)
    keep = jnp.where(first, summed[:shard], summed[shard:])
    back = swap(jnp.where(first, summed[shard:], summed[:shard]))

    parts = parts + swap(parts)
    parts = jnp.sum(spread(parts), axis=0)
    parts = swap(parts)
    parts = jnp.sum(spread(parts), axis=0)

    return (
        parts[0, 0] / (2.0 * pairs),
        jnp.where(first, keep, back),
        jnp.where(first, back, keep),
        parts[1, 0],
    )


def solution(mesh):
    in_specs = (P(("row", "col"), None), P(("col", "row"), None), P())
    out_specs = (P(), P(("row", "col"), None), P(("col", "row"), None), P())
    return jax.shard_map(
        on_device, mesh=mesh, in_specs=in_specs, out_specs=out_specs, check_vma=False
    )
```

```python
import functools
import itertools

import jax
import jax.numpy as jnp
import numpy as np
from jax import lax
from jax.experimental import pallas as pl
from jax.experimental.pallas import tpu as pltpu
from jax.sharding import PartitionSpec as P

LOG2E = 1.4426950408889634
LN2 = 0.6931471805599453
AXES = ("row", "col")
ROWS = 256
VMEM = 60 * 1024 * 1024
EXTRA = 16
CALLS = ((0, 2), (2, 5), (5, 8))


def linear(x, y, z, core):
    return (((x % 2) * 2 + core) * 4 + z) * 8 + (x // 2) * 4 + y


def devices():
    return itertools.product(range(4), range(4), range(4), range(2))


def partner_perm():
    return [(linear(x, y, z, c), linear(x, y, z, 1 - c)) for x, y, z, c in devices()]


TARGETS = ((2, 1), (2, 0), (1, 1), (-1, 1), (1, 0), (-1, 0), (0, 1), (0, 0))


def moved(x, y, z, core, steps, pair):
    if core == 0:
        return (3 - x if pair else x, (y + steps) % 4, z, core)
    return (x ^ 1 if pair else x, y, (z + steps) % 4, core)


def ring_perm(steps, pair):
    return [(linear(*d), linear(*moved(*d, steps, pair))) for d in devices()]


def group_of(x, y, z, core):
    return sorted(linear(*moved(x, y, z, core, steps, pair)) for steps, pair in TARGETS)


def groups():
    return sorted(set(tuple(group_of(*d)) for d in devices()))


def block_ids(x, y, z, core):
    out = []
    for member in group_of(x, y, z, core):
        row, col = member // 32, member % 32
        for c in (0, 1):
            at = (row // 2) * 2 + c
            out.append(at * 32 + col if core == 0 else col * 4 + at)
    return out


def tables():
    match = np.full((128, 16), -1, np.int32)
    place = np.zeros((128, 8), np.int32)
    for d in devices():
        x, y, z, c = d
        own, other = block_ids(x, y, z, c), block_ids(x, y, z, 1 - c)
        for k, block in enumerate(own):
            if block in other:
                match[linear(*d), k] = other.index(block)
        for k, (steps, pair) in enumerate(TARGETS):
            place[linear(*d), k] = group_of(*d).index(linear(*moved(*d, steps, pair)))
    return match, place


def to_column(row):
    n = row.shape[1]
    eye = lax.broadcasted_iota(jnp.int32, (n, n), 0) == lax.broadcasted_iota(jnp.int32, (n, n), 1)
    return jnp.sum(jnp.where(eye, jnp.broadcast_to(row, (n, n)), 0.0), axis=1, keepdims=True)


def to_row(column):
    n = column.shape[0]
    eye = lax.broadcasted_iota(jnp.int32, (n, n), 0) == lax.broadcasted_iota(jnp.int32, (n, n), 1)
    return jnp.sum(jnp.where(eye, jnp.broadcast_to(column, (n, n)), 0.0), axis=0, keepdims=True)


def eye(n):
    return lax.broadcasted_iota(jnp.int32, (n, n), 0) == lax.broadcasted_iota(jnp.int32, (n, n), 1)


def score_kernel(match_ref, scale_ref, own_ref, other_ref, scores_ref, stats_ref):
    step = pl.program_id(0)
    chunk = 512
    peak = total = weighted = None
    for at in range(0, other_ref.shape[0], chunk):
        scores = scale_ref[0] * lax.dot_general(
            own_ref[...],
            other_ref[at : at + chunk, :],
            (((1,), (1,)), ((), ())),
            preferred_element_type=jnp.float32,
        )
        scores_ref[:, at : at + chunk] = scores
        parts = [scores[:, k : k + 128] for k in range(0, chunk, 128)]
        top = functools.reduce(jnp.maximum, parts)
        if peak is not None:
            top = jnp.maximum(top, peak)
        powers = [jnp.exp2(part - top) for part in parts]
        new_total = functools.reduce(jnp.add, powers)
        new_weighted = functools.reduce(jnp.add, [a * b for a, b in zip(powers, parts)])
        if peak is not None:
            shrink = jnp.exp2(peak - top)
            new_total = new_total + total * shrink
            new_weighted = new_weighted + weighted * shrink
        peak, total, weighted = top, new_total, new_weighted
    top = jnp.max(peak, axis=1, keepdims=True)
    shrink = jnp.exp2(peak - top)
    stats_ref[0:1, :] = to_row(top)
    stats_ref[1:2, :] = to_row(jnp.sum(total * shrink, axis=1, keepdims=True))
    stats_ref[2:3, :] = to_row(jnp.sum(weighted * shrink, axis=1, keepdims=True))
    stats_ref[3:4, :] = jnp.zeros_like(stats_ref[3:4, :])
    for half in range(ROWS // 128):
        place = match_ref[step * (ROWS // 128) + half]

        @pl.when(place >= 0)
        def _():
            rows = slice(half * 128, half * 128 + 128)
            corner = scores_ref[rows, pl.ds(pl.multiple_of(place * 128, 128), 128)]
            stats_ref[3:4, rows] = jnp.sum(jnp.where(eye(128), corner, 0.0), axis=0, keepdims=True)


def score_call(match, scale, own, other):
    n, width = own.shape
    m = other.shape[0]
    return pl.pallas_call(
        score_kernel,
        grid=(n // ROWS,),
        in_specs=[
            pl.BlockSpec(memory_space=pltpu.SMEM),
            pl.BlockSpec(memory_space=pltpu.SMEM),
            pl.BlockSpec((ROWS, width), lambda i: (i, 0)),
            pl.BlockSpec((m, width), lambda i: (0, 0)),
        ],
        out_specs=[
            pl.BlockSpec((ROWS, m), lambda i: (i, 0)),
            pl.BlockSpec((4, ROWS), lambda i: (0, i)),
        ],
        out_shape=[
            jax.ShapeDtypeStruct((n, m), jnp.float32),
            jax.ShapeDtypeStruct((4, n), jnp.float32),
        ],
        compiler_params=pltpu.CompilerParams(vmem_limit_bytes=VMEM),
        cost_estimate=pl.CostEstimate(
            flops=2 * n * m * width, bytes_accessed=4 * n * m, transcendentals=n * m
        ),
        name="scores",
    )(match, scale, own, other)


def grad_kernel(
    pairs, count, has_own, place_ref, match_ref, scale_ref, own_lse_ref, other_lse_ref, scores_ref, other_ref, *refs
):
    outs = refs[:count]
    weights, blocks, own, other, out_sems, other_sem = refs[count:]
    step = pl.program_id(0)
    m = other.shape[0]
    load_other = pltpu.make_async_copy(other_ref, other, other_sem)
    stores = [
        pltpu.make_async_copy(own if has_own and k == count - 1 else blocks.at[k], outs[k], out_sems.at[k])
        for k in range(count)
    ]

    @pl.when(step == 0)
    def _():
        load_other.start()

    begin = pl.multiple_of(place_ref[step] * ROWS, ROWS)
    own_lse = to_column(own_lse_ref[:, pl.ds(begin, ROWS)])
    for at in range(0, m, 512):
        part = scores_ref[:, at : at + 512]
        weights[:, at : at + 512] = (
            jnp.exp2(part - own_lse) + jnp.exp2(part - other_lse_ref[:, at : at + 512])
        ).astype(jnp.bfloat16)
    for half in range(ROWS // 128):
        place = match_ref[place_ref[step] * (ROWS // 128) + half]

        @pl.when(place >= 0)
        def _():
            rows = slice(half * 128, half * 128 + 128)
            columns = pl.ds(pl.multiple_of(place * 128, 128), 128)
            corner = scores_ref[rows, columns]
            weight = jnp.exp2(corner - own_lse[rows]) + jnp.exp2(corner - other_lse_ref[:, columns])
            weights[rows, columns] = (weight - jnp.where(eye(128), 1.0 / pairs, 0.0)).astype(jnp.bfloat16)

    @pl.when(step == 0)
    def _():
        load_other.wait()

    grad = scale_ref[0] * jnp.dot(weights[...], other[...], preferred_element_type=jnp.float32)
    blocks[step, 0:ROWS, :] = grad.astype(jnp.bfloat16)
    if has_own:
        own[...] = grad
    parts = other_lse_ref[:, m : m + 256]
    high = parts.astype(jnp.bfloat16).astype(jnp.float32)
    middle = (parts - high).astype(jnp.bfloat16).astype(jnp.float32)
    row = lax.broadcasted_iota(jnp.int32, (EXTRA, 256), 0)
    rows = [jnp.broadcast_to(v, (EXTRA, 256)) for v in (high, middle, parts - high - middle)]
    tile = jnp.where(row == 0, rows[0], jnp.where(row == 1, rows[1], jnp.where(row == 2, rows[2], 0.0)))
    blocks[step, ROWS:, :] = jnp.zeros((EXTRA, blocks.shape[2]), jnp.bfloat16)
    blocks[step, ROWS:, 0:256] = tile.astype(jnp.bfloat16)
    for k in range(count):

        @pl.when(step == k)
        def _():
            stores[k].start()

    @pl.when(step == count - 1)
    def _():
        for store in stores:
            store.wait()


def grad_call(pairs, targets, places, match, scale, scores, own_lse, other_lse, other):
    m, width = other.shape
    count = len(targets)
    has_own = targets[-1] == (0, 0)
    smem, vmem, anywhere = (pl.BlockSpec(memory_space=s) for s in (pltpu.SMEM, pltpu.VMEM, pl.ANY))
    sent = jax.ShapeDtypeStruct((ROWS + EXTRA, width), jnp.bfloat16)
    kept = jax.ShapeDtypeStruct((ROWS, width), jnp.float32)
    return pl.pallas_call(
        functools.partial(grad_kernel, pairs, count, has_own),
        grid_spec=pltpu.PrefetchScalarGridSpec(
            num_scalar_prefetch=1,
            grid=(count,),
            in_specs=[
                smem,
                smem,
                vmem,
                vmem,
                pl.BlockSpec((ROWS, m), lambda i, place: (place[i], 0)),
                anywhere,
            ],
            out_specs=[anywhere] * count,
            scratch_shapes=[
                pltpu.VMEM((ROWS, m), jnp.bfloat16),
                pltpu.VMEM((count, ROWS + EXTRA, width), jnp.bfloat16),
                pltpu.VMEM((ROWS, width), jnp.float32),
                pltpu.VMEM((m, width), jnp.bfloat16),
                pltpu.SemaphoreType.DMA((count,)),
                pltpu.SemaphoreType.DMA,
            ],
        ),
        out_shape=[kept if has_own and k == count - 1 else sent for k in range(count)],
        compiler_params=pltpu.CompilerParams(vmem_limit_bytes=VMEM),
        cost_estimate=pl.CostEstimate(
            flops=2 * count * ROWS * m * width,
            bytes_accessed=4 * count * ROWS * m,
            transcendentals=2 * count * ROWS * m,
        ),
        name="grads",
    )(places, match, scale, own_lse, other_lse, scores, other)


def on_device(images, texts, logit_scale):
    shard, width = images.shape
    pairs = shard * 128
    me = lax.axis_index(AXES)
    first = lax.rem(lax.axis_index("row"), 2) == 0
    swap = functools.partial(lax.ppermute, axis_name=AXES, perm=partner_perm())
    members = [list(g) for g in groups()]
    match, place = (lax.dynamic_slice(jnp.asarray(t), (me, 0), (1, t.shape[1])).reshape(-1) for t in tables())

    def spread(value):
        everywhere = jnp.broadcast_to(value[None], (8,) + value.shape)
        return lax.all_to_all(everywhere, AXES, 0, 0, axis_index_groups=members, tiled=True)

    got = swap(jnp.where(first, texts, images))
    mine = jnp.where(first, images, texts)
    chip = jnp.concatenate([jnp.where(first, mine, got), jnp.where(first, got, mine)], axis=0)
    own = spread(chip).reshape(16 * shard, width)
    other = swap(own)

    scale2 = (logit_scale * LOG2E).reshape(1)
    scores, stats = score_call(match, scale2, own, other)
    peaks, totals, weighted, matched = (spread(stats)[:, k] for k in range(4))
    peak = jnp.max(peaks, axis=0, keepdims=True)
    shrink = jnp.exp2(peaks - peak)
    total = jnp.sum(totals * shrink, axis=0, keepdims=True)
    shift = float(np.log2(2.0 * pairs))
    own_lse = peak + jnp.log2(total) + shift

    diagonal = jnp.sum(matched)
    mean_score = jnp.sum(jnp.sum(weighted * shrink, axis=0, keepdims=True) / total)
    parts = [jnp.sum(own_lse - shift) - diagonal, mean_score - diagonal]
    other_lse = swap(jnp.concatenate([own_lse] + [jnp.broadcast_to(v, (1, 128)) for v in parts], axis=1))

    received = []
    kept = None
    for begin, end in CALLS:
        targets = TARGETS[begin:end]
        out = grad_call(
            pairs, targets, place[begin:end], match, logit_scale.reshape(1), scores, own_lse, other_lse, other
        )
        for target, grad in zip(targets, out):
            if target == (0, 0):
                kept = grad
            else:
                received.append(lax.ppermute(grad, AXES, ring_perm(*target)))
    received = [v.astype(jnp.float32) for v in received]
    summed = functools.reduce(jnp.add, [v[:ROWS] for v in received]) + kept
    parts = functools.reduce(jnp.add, [jnp.sum(v[ROWS : ROWS + 3, 0:256], axis=0, keepdims=True) for v in received])
    parts = parts + other_lse[:, 16 * shard :]
    parts = jnp.pad(parts, ((0, 7), (0, width - 256)))
    keep = jnp.where(first, summed[:shard], summed[shard:])
    back = swap(jnp.concatenate([jnp.where(first, summed[shard:], summed[:shard]), parts], axis=0))
    parts = (parts[0] + back[shard]) * (LN2 / (2.0 * pairs))
    return (
        parts[0],
        jnp.where(first, keep, back[:shard]),
        jnp.where(first, back[:shard], keep),
        parts[128] / logit_scale,
    )


def solution(mesh):
    in_specs = (P(("row", "col"), None), P(("col", "row"), None), P())
    out_specs = (P(), P(("row", "col"), None), P(("col", "row"), None), P())
    return jax.shard_map(
        on_device, mesh=mesh, in_specs=in_specs, out_specs=out_specs, check_vma=False
    )
```

```python
import functools
import itertools

import jax
import jax.numpy as jnp
import numpy as np
from jax import lax
from jax.experimental import pallas as pl
from jax.experimental.pallas import tpu as pltpu
from jax.sharding import PartitionSpec as P

LOG2E = 1.4426950408889634
LN2 = 0.6931471805599453
AXES = ("row", "col")
ROWS = 256
VMEM = 63_400_000
EXTRA = 16
PAIR = 2


def linear(x, y, z, core):
    return (((x % 2) * 2 + core) * 4 + z) * 8 + (x // 2) * 4 + y


def devices():
    return itertools.product(range(4), range(4), range(4), range(2))


def partner_perm():
    return [(linear(x, y, z, c), linear(x, y, z, 1 - c)) for x, y, z, c in devices()]


PIECES = ((0, 0), (1, 0), (-1, 0), (0, 1), (2, 0), (-1, 1), (1, 1), (2, 1))


def moved(x, y, z, core, steps, pair):
    if core == 0:
        return (3 - x if pair else x, (y + steps) % 4, z, core)
    return (x ^ 1 if pair else x, y, (z + steps) % 4, core)


def ring_perm(steps, pair):
    return [(linear(*d), linear(*moved(*d, steps, pair))) for d in devices()]


def group_of(x, y, z, core):
    return sorted(linear(*moved(x, y, z, core, steps, pair)) for steps, pair in PIECES)


def groups():
    return sorted(set(tuple(group_of(*d)) for d in devices()))


def block_ids(x, y, z, core):
    out = []
    for steps, pair in PIECES:
        member = linear(*moved(x, y, z, core, steps, pair))
        row, col = member // 32, member % 32
        for c in (0, 1):
            at = (row // 2) * 2 + c
            out.append(at * 32 + col if core == 0 else col * 4 + at)
    return out


def tables():
    table = np.full((128, 32), -1, np.int32)
    for d in devices():
        x, y, z, c = d
        own, other = block_ids(x, y, z, c), block_ids(x, y, z, 1 - c)
        for k, block in enumerate(own):
            if block in other:
                table[linear(*d), k] = other.index(block)
        for side in (0, 1):
            e = (x, y, z, c ^ side)
            for k, (steps, pair) in enumerate(PIECES):
                table[linear(*d), 16 + 8 * side + k] = group_of(*e).index(linear(*moved(*e, steps, pair)))
    return table


def to_column(row):
    n = row.shape[1]
    eye = lax.broadcasted_iota(jnp.int32, (n, n), 0) == lax.broadcasted_iota(jnp.int32, (n, n), 1)
    return jnp.sum(jnp.where(eye, jnp.broadcast_to(row, (n, n)), 0.0), axis=1, keepdims=True)


def eye(n):
    return lax.broadcasted_iota(jnp.int32, (n, n), 0) == lax.broadcasted_iota(jnp.int32, (n, n), 1)


def fetch(parts, whole, sems):
    return [
        pltpu.make_async_copy(part, whole.at[pl.ds(k * ROWS, ROWS)], sems.at[k]) for k, part in enumerate(parts)
    ]


def table_place(table_ref, side, piece):
    return pl.multiple_of(table_ref[16 + 8 * side + piece] * ROWS, ROWS)


def tile_stats(scale, rows, other_at, width, scores_ref):
    chunk = 512 if width % 512 == 0 else 256
    peak = total = weighted = None
    for at in range(0, width, chunk):
        scores = scale * lax.dot_general(
            rows, other_at(at, chunk), (((1,), (1,)), ((), ())), preferred_element_type=jnp.float32
        )
        scores_ref[:, at : at + chunk] = scores
        parts = [scores[:, k : k + 128] for k in range(0, chunk, 128)]
        top = functools.reduce(jnp.maximum, parts)
        if peak is not None:
            top = jnp.maximum(top, peak)
        powers = [jnp.exp2(part - top) for part in parts]
        new_total = functools.reduce(jnp.add, powers)
        new_weighted = functools.reduce(jnp.add, [a * b for a, b in zip(powers, parts)])
        if peak is not None:
            shrink = jnp.exp2(peak - top)
            new_total = new_total + total * shrink
            new_weighted = new_weighted + weighted * shrink
        peak, total, weighted = top, new_total, new_weighted
    peak = peak.T
    top = jnp.max(peak, axis=0, keepdims=True)
    shrink = jnp.exp2(peak - top)
    return (
        top,
        jnp.sum(total.T * shrink, axis=0, keepdims=True),
        jnp.sum(weighted.T * shrink, axis=0, keepdims=True),
    )


def put_matched(table_ref, piece, begin, width, scores_ref, line):
    line[3:4, :] = jnp.zeros((1, ROWS), jnp.float32)
    for half in range(ROWS // 128):
        place = table_ref[piece * (ROWS // 128) + half] * 128 - begin

        @pl.when(jnp.logical_and(place >= 0, place < width))
        def _():
            span = slice(half * 128, half * 128 + 128)
            corner = scores_ref[span, pl.ds(pl.multiple_of(place, 128), 128)]
            line[3:4, span] = jnp.sum(jnp.where(eye(128), corner, 0.0), axis=0, keepdims=True)


def score_kernel(n, table_ref, scale_ref, *refs):
    own_refs, other_refs = refs[:n], refs[n : 2 * n]
    scores_ref, stats_ref, own, other, line, own_sems, other_sems = refs[2 * n :]
    step = pl.program_id(0)
    load_own, load_other = fetch(own_refs, own, own_sems), fetch(other_refs, other, other_sems)

    @pl.when(step == 0)
    def _():
        for copy in load_own[:1] + load_other + load_own[1:]:
            copy.start()
        for copy in load_own[:1] + load_other:
            copy.wait()

    @pl.when(step == 1)
    def _():
        for copy in load_own[1:]:
            copy.wait()

    rows = own[pl.ds(pl.multiple_of(step * ROWS, ROWS), ROWS), :]
    width = n * ROWS
    top, total, weighted = tile_stats(
        scale_ref[0], rows, lambda at, chunk: other[at : at + chunk, :], width, scores_ref
    )
    line[0:1, :] = top
    line[1:2, :] = total
    line[2:3, :] = weighted
    put_matched(table_ref, step, 0, width, scores_ref, line)
    stats_ref[...] = line[...]


def score_call(table, scale, own, other):
    n, width = len(own), own[0].shape[1]
    smem, anywhere = pl.BlockSpec(memory_space=pltpu.SMEM), pl.BlockSpec(memory_space=pl.ANY)
    return pl.pallas_call(
        functools.partial(score_kernel, n),
        grid=(n,),
        in_specs=[smem, smem] + [anywhere] * (2 * n),
        out_specs=[
            pl.BlockSpec((ROWS, n * ROWS), lambda i: (i, 0)),
            pl.BlockSpec((4, ROWS), lambda i: (0, i)),
        ],
        out_shape=[
            jax.ShapeDtypeStruct(((n + 1) * ROWS, (n + 1) * ROWS), jnp.float32),
            jax.ShapeDtypeStruct((4, n * ROWS), jnp.float32),
        ],
        scratch_shapes=[
            pltpu.VMEM((n * ROWS, width), jnp.bfloat16),
            pltpu.VMEM((n * ROWS, width), jnp.bfloat16),
            pltpu.VMEM((4, ROWS), jnp.float32),
            pltpu.SemaphoreType.DMA((n,)),
            pltpu.SemaphoreType.DMA((n,)),
        ],
        compiler_params=pltpu.CompilerParams(vmem_limit_bytes=VMEM),
        cost_estimate=pl.CostEstimate(
            flops=2 * n * n * ROWS * ROWS * width,
            bytes_accessed=4 * n * n * ROWS * ROWS,
            transcendentals=n * n * ROWS * ROWS,
        ),
        name="scores",
    )(table, scale, *own, *other)


def last_score_kernel(n, table_ref, scale_ref, before_ref, scores_in, *refs):
    own_refs, other_refs = refs[: n + 1], refs[n + 1 : 2 * n + 2]
    scores_out, stats_ref, own, other, row, column, line, own_sems, other_sems, out_sems = refs[2 * n + 2 :]
    load_own, load_other = fetch(own_refs, own, own_sems), fetch(other_refs, other, other_sems)
    for copy in load_own[n:] + load_other + load_own[:n]:
        copy.start()
    store_row = pltpu.make_async_copy(row, scores_out.at[pl.ds(n * ROWS, ROWS)], out_sems.at[n])
    store_column = [
        pltpu.make_async_copy(
            column.at[pl.ds(k * ROWS, ROWS)],
            scores_out.at[pl.ds(k * ROWS, ROWS), pl.ds(n * ROWS, ROWS)],
            out_sems.at[k],
        )
        for k in range(n)
    ]

    def put(piece):
        for member in range(8):
            stats_ref[member, :, pl.ds(table_place(table_ref, 0, piece), ROWS)] = line[...]

    def arrived(at, size):
        for k in range(at // ROWS, (at + size) // ROWS):
            load_other[k].wait()
        return other[at : at + size, :]

    load_own[n].wait()
    top, total, weighted = tile_stats(scale_ref[0], own[n * ROWS : (n + 1) * ROWS, :], arrived, (n + 1) * ROWS, row)
    line[0:1, :] = top
    line[1:2, :] = total
    line[2:3, :] = weighted
    put_matched(table_ref, n, 0, (n + 1) * ROWS, row, line)
    store_row.start()
    put(n)
    for copy in load_own[:n]:
        copy.wait()
    found = []
    for k in range(n):
        found.append(
            tile_stats(
                scale_ref[0],
                own[k * ROWS : (k + 1) * ROWS, :],
                lambda at, chunk: other[n * ROWS + at : n * ROWS + at + chunk, :],
                ROWS,
                column.at[pl.ds(k * ROWS, ROWS)],
            )
        )
    for k, (top, total, weighted) in enumerate(found):
        store_column[k].start()
        put_matched(table_ref, k, n * ROWS, ROWS, column.at[pl.ds(k * ROWS, ROWS)], line)
        old = before_ref[:, k * ROWS : (k + 1) * ROWS]
        new_top = jnp.maximum(old[0:1], top)
        old_shrink, new_shrink = jnp.exp2(old[0:1] - new_top), jnp.exp2(top - new_top)
        line[0:1, :] = new_top
        line[1:2, :] = old[1:2] * old_shrink + total * new_shrink
        line[2:3, :] = old[2:3] * old_shrink + weighted * new_shrink
        line[3:4, :] = old[3:4] + line[3:4, :]
        put(k)
    store_row.wait()
    for store in store_column:
        store.wait()


def last_score_call(table, scale, before, scores, own, other):
    n, width = len(own) - 1, own[0].shape[1]
    smem, vmem, anywhere = (pl.BlockSpec(memory_space=s) for s in (pltpu.SMEM, pltpu.VMEM, pl.ANY))
    rows = (n + 1) * ROWS
    return pl.pallas_call(
        functools.partial(last_score_kernel, n),
        in_specs=[smem, smem, vmem] + [anywhere] * (2 * n + 3),
        out_specs=[anywhere, vmem],
        out_shape=[
            jax.ShapeDtypeStruct(scores.shape, jnp.float32),
            jax.ShapeDtypeStruct((8, 4, rows), jnp.float32),
        ],
        scratch_shapes=[
            pltpu.VMEM((rows, width), jnp.bfloat16),
            pltpu.VMEM((rows, width), jnp.bfloat16),
            pltpu.VMEM((ROWS, rows), jnp.float32),
            pltpu.VMEM((n * ROWS, ROWS), jnp.float32),
            pltpu.VMEM((4, ROWS), jnp.float32),
            pltpu.SemaphoreType.DMA((n + 1,)),
            pltpu.SemaphoreType.DMA((n + 1,)),
            pltpu.SemaphoreType.DMA((n + 1,)),
        ],
        input_output_aliases={3: 0},
        compiler_params=pltpu.CompilerParams(vmem_limit_bytes=VMEM),
        cost_estimate=pl.CostEstimate(
            flops=2 * (2 * n + 1) * ROWS * ROWS * width,
            bytes_accessed=4 * (2 * n + 1) * ROWS * ROWS,
            transcendentals=(2 * n + 1) * ROWS * ROWS,
        ),
        name="last_scores",
    )(table, scale, before, scores, *own, *other)


def join_kernel(shift, stats_ref, out_ref):
    rows = out_ref.shape[1] - 256
    peak = functools.reduce(jnp.maximum, [stats_ref[k, 0:1, :] for k in range(8)])
    total = weighted = matched = 0.0
    for k in range(8):
        shrink = jnp.exp2(stats_ref[k, 0:1, :] - peak)
        total = total + stats_ref[k, 1:2, :] * shrink
        weighted = weighted + stats_ref[k, 2:3, :] * shrink
        matched = matched + stats_ref[k, 3:4, :]
    lse = peak + jnp.log2(total)
    out_ref[:, :rows] = lse + shift
    for k, value in enumerate((lse - matched, weighted / total - matched)):
        value = jnp.sum(value, axis=1, keepdims=True)
        out_ref[:, rows + 128 * k : rows + 128 * (k + 1)] = jnp.broadcast_to(value, (1, 128))


def join_call(shift, stats):
    return pl.pallas_call(
        functools.partial(join_kernel, shift),
        out_shape=jax.ShapeDtypeStruct((1, stats.shape[2] + 256), jnp.float32),
        name="join",
    )(stats)


def grad_kernel(pairs, pieces, table_ref, scale_ref, own_lse_ref, other_lse_ref, scores_ref, *refs):
    count = len(pieces)
    other_refs, outs = refs[:8], refs[8 : 8 + count]
    weights, (blocks, own, other, out_sems, other_sem) = refs[8 + count : 8 + count + PAIR], refs[8 + count + PAIR :]
    step = pl.program_id(0)
    m = scores_ref.shape[1]
    load_other = fetch(other_refs, other, other_sem)
    stores = [
        pltpu.make_async_copy(own if q == 0 else blocks.at[k], outs[k], out_sems.at[k])
        for k, q in enumerate(pieces)
    ]

    @pl.when(step == 0)
    def _():
        for copy in load_other:
            copy.start()

    extra = other_lse_ref[:, m : m + 256]
    high = extra.astype(jnp.bfloat16).astype(jnp.float32)
    middle = (extra - high).astype(jnp.bfloat16).astype(jnp.float32)
    row = lax.broadcasted_iota(jnp.int32, (EXTRA, 256), 0)
    rows = [jnp.broadcast_to(v, (EXTRA, 256)) for v in (high, middle, extra - high - middle)]
    tile = jnp.where(row == 0, rows[0], jnp.where(row == 1, rows[1], jnp.where(row == 2, rows[2], 0.0)))
    ones = eye(128).astype(jnp.float32)

    def weigh(k):
        piece = pieces[k] - PAIR * step
        own_lse = to_column(own_lse_ref[:, pl.ds(table_place(table_ref, 0, piece), ROWS)])
        at_row = (PAIR - 1 - k) * ROWS
        found = [table_ref[piece * (ROWS // 128) + half] for half in range(ROWS // 128)]
        for at in range(0, m, ROWS):
            part = scores_ref[at_row : at_row + ROWS, at : at + ROWS]
            other_lse = other_lse_ref[:, pl.ds(table_place(table_ref, 1, at // ROWS), ROWS)]
            weight = jnp.exp2(part - own_lse) + jnp.exp2(part - other_lse)
            for i in range(0, ROWS, 128):
                for j in range(0, ROWS, 128):
                    taken = jnp.where(found[i // 128] == (at + j) // 128, 1.0 / pairs, 0.0)
                    weights[k][i : i + 128, at + j : at + j + 128] = (
                        weight[i : i + 128, j : j + 128] - ones * taken
                    ).astype(jnp.bfloat16)

    def multiply(k):
        grad = scale_ref[0] * jnp.dot(weights[k][...], other[...], preferred_element_type=jnp.float32)
        slot = PAIR * step + k
        blocks[slot, 0:ROWS, :] = grad.astype(jnp.bfloat16)
        blocks[slot, ROWS:, :] = jnp.zeros((EXTRA, blocks.shape[2]), jnp.bfloat16)
        blocks[slot, ROWS:, 0:256] = tile.astype(jnp.bfloat16)
        if pieces[-1] == 0 and k == PAIR - 1:
            own[...] = grad

    weigh(0)

    @pl.when(step == 0)
    def _():
        for copy in load_other:
            copy.wait()

    multiply(0)
    for k in range(1, PAIR):
        weigh(k)
        multiply(k)
    for at in range(0, count, PAIR):

        @pl.when(step == at // PAIR)
        def _():
            for k in range(at, at + PAIR):
                stores[k].start()

    @pl.when(step == count // PAIR - 1)
    def _():
        for store in stores:
            store.wait()


def grad_call(name, pairs, pieces, table, scale, scores, own_lse, other_lse, other):
    width = other[0].shape[1]
    count = len(pieces)
    m = scores.shape[1]
    smem, vmem, anywhere = (pl.BlockSpec(memory_space=s) for s in (pltpu.SMEM, pltpu.VMEM, pl.ANY))
    sent = jax.ShapeDtypeStruct((ROWS + EXTRA, width), jnp.bfloat16)
    kept = jax.ShapeDtypeStruct((ROWS, width), jnp.float32)
    return pl.pallas_call(
        functools.partial(grad_kernel, pairs, pieces),
        grid=(count // PAIR,),
        in_specs=[
            smem,
            smem,
            vmem,
            vmem,
            pl.BlockSpec((PAIR * ROWS, m), lambda i: (pieces[0] // PAIR - i, 0)),
        ]
        + [anywhere] * 8,
        out_specs=[anywhere] * count,
        out_shape=[kept if q == 0 else sent for q in pieces],
        scratch_shapes=[pltpu.VMEM((ROWS, m), jnp.bfloat16)] * PAIR
        + [
            pltpu.VMEM((count, ROWS + EXTRA, width), jnp.bfloat16),
            pltpu.VMEM((ROWS, width), jnp.float32),
            pltpu.VMEM((m, width), jnp.bfloat16),
            pltpu.SemaphoreType.DMA((count,)),
            pltpu.SemaphoreType.DMA((8,)),
        ],
        compiler_params=pltpu.CompilerParams(vmem_limit_bytes=VMEM),
        cost_estimate=pl.CostEstimate(
            flops=2 * count * ROWS * m * width,
            bytes_accessed=4 * count * ROWS * m,
            transcendentals=2 * count * ROWS * m,
        ),
        name=name,
    )(table, scale, own_lse, other_lse, scores, *other)


def on_device(images, texts, logit_scale):
    shard, width = images.shape
    pairs = shard * 128
    me = lax.axis_index(AXES)
    first = lax.rem(lax.axis_index("row"), 2) == 0
    swap = functools.partial(lax.ppermute, axis_name=AXES, perm=partner_perm())
    members = [list(g) for g in groups()]
    table = lax.dynamic_slice(jnp.asarray(tables()), (me, 0), (1, 32)).reshape(-1)
    scale2 = (logit_scale * LOG2E).reshape(1)

    def send(value, steps, pair):
        return lax.ppermute(value, AXES, ring_perm(steps, pair))

    got = swap(jnp.where(first, texts, images))
    mine = jnp.where(first, images, texts)
    chip = jnp.concatenate([jnp.where(first, mine, got), jnp.where(first, got, mine)], axis=0)

    after, before, across = send(chip, -1, 0), send(chip, 1, 0), send(chip, 0, 1)
    near = [chip, after, before, across]
    middle = [send(after, -1, 0), send(across, 1, 0), send(after, 0, 1)]
    far = send(middle[2], -1, 0)
    own = near + middle
    other = [swap(v) for v in own]
    scores, stats = score_call(table, scale2, own, other)
    stats, far = lax.optimization_barrier((stats, far))
    other = other + [swap(far)]
    scores, stats = last_score_call(table, scale2, stats, scores, own + [far], other)

    spread = lax.all_to_all(stats, AXES, 0, 0, axis_index_groups=members, tiled=True)
    own_lse = join_call(float(np.log2(2.0 * pairs)), spread)
    other_lse = swap(own_lse)

    def grads(name, pieces):
        return grad_call(name, pairs, pieces, table, logit_scale.reshape(1), scores, own_lse, other_lse, other)

    received = [send(v, *PIECES[q]) for q, v in zip((7, 6, 5, 4), grads("grads_far", (7, 6, 5, 4)))]
    *near_grads, kept = grads("grads_near", (3, 2, 1, 0))
    received, near_grads = lax.optimization_barrier((received, near_grads))
    received += [send(v, *PIECES[q]) for q, v in zip((3, 2, 1), near_grads)]
    received = [v.astype(jnp.float32) for v in received]
    summed = functools.reduce(jnp.add, [v[:ROWS] for v in received]) + kept
    parts = functools.reduce(jnp.add, [jnp.sum(v[ROWS : ROWS + 3, 0:256], axis=0, keepdims=True) for v in received])
    parts = parts + other_lse[:, 16 * shard :]
    parts = jnp.pad(parts, ((0, 7), (0, width - 256)))
    keep = jnp.where(first, summed[:shard], summed[shard:])
    back = swap(jnp.concatenate([jnp.where(first, summed[shard:], summed[:shard]), parts], axis=0))
    parts = (parts[0] + back[shard]) * (LN2 / (2.0 * pairs))
    return (
        parts[0],
        jnp.where(first, keep, back[:shard]),
        jnp.where(first, back[:shard], keep),
        parts[128] / logit_scale,
    )


def solution(mesh):
    in_specs = (P(("row", "col"), None), P(("col", "row"), None), P())
    out_specs = (P(), P(("row", "col"), None), P(("col", "row"), None), P())
    return jax.shard_map(
        on_device, mesh=mesh, in_specs=in_specs, out_specs=out_specs, check_vma=False
    )
```

```python
import functools
import itertools

import jax
import jax.numpy as jnp
import numpy as np
from jax import lax
from jax.experimental import pallas as pl
from jax.experimental.pallas import tpu as pltpu
from jax.sharding import PartitionSpec as P

LOG2E = 1.4426950408889634
LN2 = 0.6931471805599453
AXES = ("row", "col")
ROWS = 256
VMEM = 24 * 1024 * 1024
SPARE = 3328
EXTRA = 16
PAIR = 2


def linear(x, y, z, core):
    return (((x % 2) * 2 + core) * 4 + z) * 8 + (x // 2) * 4 + y


def devices():
    return itertools.product(range(4), range(4), range(4), range(2))


def partner_perm():
    return [(linear(x, y, z, c), linear(x, y, z, 1 - c)) for x, y, z, c in devices()]


PIECES = ((0, 0), (1, 0), (-1, 0), (0, 1), (2, 0), (-1, 1), (1, 1), (2, 1))


def moved(x, y, z, core, steps, pair):
    if core == 0:
        return (3 - x if pair else x, (y + steps) % 4, z, core)
    return (x ^ 1 if pair else x, y, (z + steps) % 4, core)


def ring_perm(steps, pair):
    return [(linear(*d), linear(*moved(*d, steps, pair))) for d in devices()]


def group_of(x, y, z, core):
    return sorted(linear(*moved(x, y, z, core, steps, pair)) for steps, pair in PIECES)


def groups():
    return sorted(set(tuple(group_of(*d)) for d in devices()))


def block_ids(x, y, z, core):
    out = []
    for steps, pair in PIECES:
        member = linear(*moved(x, y, z, core, steps, pair))
        row, col = member // 32, member % 32
        for c in (0, 1):
            at = (row // 2) * 2 + c
            out.append(at * 32 + col if core == 0 else col * 4 + at)
    return out


def tables():
    table = np.full((128, 32), -1, np.int32)
    for d in devices():
        x, y, z, c = d
        own, other = block_ids(x, y, z, c), block_ids(x, y, z, 1 - c)
        for k, block in enumerate(own):
            if block in other:
                table[linear(*d), k] = other.index(block)
        for side in (0, 1):
            e = (x, y, z, c ^ side)
            for k, (steps, pair) in enumerate(PIECES):
                table[linear(*d), 16 + 8 * side + k] = group_of(*e).index(linear(*moved(*e, steps, pair)))
    return table


def to_column(row):
    n = row.shape[1]
    eye = lax.broadcasted_iota(jnp.int32, (n, n), 0) == lax.broadcasted_iota(jnp.int32, (n, n), 1)
    return jnp.sum(jnp.where(eye, jnp.broadcast_to(row, (n, n)), 0.0), axis=1, keepdims=True)


def eye(n):
    return lax.broadcasted_iota(jnp.int32, (n, n), 0) == lax.broadcasted_iota(jnp.int32, (n, n), 1)


def fetch(parts, whole, sems):
    return [
        pltpu.make_async_copy(part, whole.at[pl.ds(k * ROWS, ROWS)], sems.at[k]) for k, part in enumerate(parts)
    ]


def table_place(table_ref, side, piece):
    return pl.multiple_of(table_ref[16 + 8 * side + piece] * ROWS, ROWS)


def tile_stats(scale, rows, other_at, width, scores_ref):
    chunk = 512 if width % 512 == 0 else 256
    peak = total = weighted = None
    for at in range(0, width, chunk):
        scores = scale * lax.dot_general(
            rows, other_at(at, chunk), (((1,), (1,)), ((), ())), preferred_element_type=jnp.float32
        )
        scores_ref[:, at : at + chunk] = scores
        parts = [scores[:, k : k + 128] for k in range(0, chunk, 128)]
        top = functools.reduce(jnp.maximum, parts)
        if peak is not None:
            top = jnp.maximum(top, peak)
        powers = [jnp.exp2(part - top) for part in parts]
        new_total = functools.reduce(jnp.add, powers)
        new_weighted = functools.reduce(jnp.add, [a * b for a, b in zip(powers, parts)])
        if peak is not None:
            shrink = jnp.exp2(peak - top)
            new_total = new_total + total * shrink
            new_weighted = new_weighted + weighted * shrink
        peak, total, weighted = top, new_total, new_weighted
    peak = peak.T
    top = jnp.max(peak, axis=0, keepdims=True)
    shrink = jnp.exp2(peak - top)
    return (
        top,
        jnp.sum(total.T * shrink, axis=0, keepdims=True),
        jnp.sum(weighted.T * shrink, axis=0, keepdims=True),
    )


def put_matched(table_ref, piece, begin, width, scores_ref, line):
    line[3:4, :] = jnp.zeros((1, ROWS), jnp.float32)
    for half in range(ROWS // 128):
        place = table_ref[piece * (ROWS // 128) + half] * 128 - begin

        @pl.when(jnp.logical_and(place >= 0, place < width))
        def _():
            span = slice(half * 128, half * 128 + 128)
            corner = scores_ref[span, pl.ds(pl.multiple_of(place, 128), 128)]
            line[3:4, span] = jnp.sum(jnp.where(eye(128), corner, 0.0), axis=0, keepdims=True)


def score_kernel(old, new, last, table_ref, scale_ref, *refs):
    total = old + new
    if old:
        before_ref, refs = refs[0], refs[2:]
    own_refs, other_refs = refs[:total], refs[total : 2 * total]
    scores_out, stats_ref, own, other, row, column, line, own_sems, other_sems, out_sems = refs[2 * total :]
    load_own, load_other = fetch(own_refs, own, own_sems), fetch(other_refs, other, other_sems)
    for copy in load_own[old:] + load_other + load_own[:old]:
        copy.start()

    def piece_rows(k):
        return pl.ds(k * ROWS if isinstance(k, int) else pl.multiple_of(k * ROWS, ROWS), ROWS)

    def store_old(k):
        return pltpu.make_async_copy(
            column.at[piece_rows(k)],
            scores_out.at[piece_rows(k), pl.ds(old * ROWS, new * ROWS)],
            out_sems.at[k],
        )

    def store_new(k):
        return pltpu.make_async_copy(
            row.at[piece_rows(k)],
            scores_out.at[piece_rows(k + old), pl.ds(0, total * ROWS)],
            out_sems.at[k + old],
        )

    def put(piece, top, power, weighted):
        line[0:1, :] = top
        line[1:2, :] = power
        line[2:3, :] = weighted
        if last:
            for member in range(8):
                stats_ref[member, :, pl.ds(table_place(table_ref, 0, piece), ROWS)] = line[...]
        else:
            stats_ref[:, piece_rows(piece)] = line[...]

    def part(at, size):
        if new == 1:
            for k in range(at // ROWS, (at + size) // ROWS):
                load_other[k].wait()
        return other[at : at + size, :]

    def new_piece(k):
        target = row.at[piece_rows(k)]
        top, power, weighted = tile_stats(scale_ref[0], own[piece_rows(k + old), :], part, total * ROWS, target)
        store_new(k).start()
        put_matched(table_ref, k + old, 0, total * ROWS, target, line)
        put(k + old, top, power, weighted)

    def old_scores(k):
        stats = tile_stats(
            scale_ref[0],
            own[piece_rows(k), :],
            lambda at, size: other[old * ROWS + at : old * ROWS + at + size, :],
            new * ROWS,
            column.at[piece_rows(k)],
        )
        store_old(k).start()
        return stats

    def old_stats(k, top, power, weighted):
        put_matched(table_ref, k, old * ROWS, new * ROWS, column.at[piece_rows(k)], line)
        earlier = before_ref[:, piece_rows(k)]
        new_top = jnp.maximum(earlier[0:1], top)
        old_shrink, new_shrink = jnp.exp2(earlier[0:1] - new_top), jnp.exp2(top - new_top)
        line[3:4, :] = earlier[3:4] + line[3:4, :]
        put(k, new_top, earlier[1:2] * old_shrink + power * new_shrink, earlier[2:3] * old_shrink + weighted * new_shrink)

    for copy in load_own[old:] + (load_other if new > 1 else []):
        copy.wait()
    if new == 1:
        new_piece(0)
    else:
        pl.loop(0, new)(new_piece)
    for copy in load_own[:old]:
        copy.wait()
    if new == 1:
        found = [old_scores(k) for k in range(old)]
        for k, stats in enumerate(found):
            old_stats(k, *stats)
    elif old:
        pl.loop(0, old)(lambda k: old_stats(k, *old_scores(k)))
    for k in range(old):
        store_old(k).wait()
    for k in range(new):
        store_new(k).wait()


def score_call(name, last, table, scale, before, own, other):
    total, width = len(own), own[0].shape[1]
    old = before[0].shape[1] // ROWS if before else 0
    new = total - old
    smem, vmem, anywhere = (pl.BlockSpec(memory_space=s) for s in (pltpu.SMEM, pltpu.VMEM, pl.ANY))
    tiles = new * total + old * new
    return pl.pallas_call(
        functools.partial(score_kernel, old, new, last),
        in_specs=[smem, smem] + ([vmem, anywhere] if before else []) + [anywhere] * (2 * total),
        out_specs=[anywhere, vmem],
        out_shape=[
            jax.ShapeDtypeStruct((8 * ROWS + SPARE, 8 * ROWS), jnp.float32),
            jax.ShapeDtypeStruct((8, 4, total * ROWS) if last else (4, total * ROWS), jnp.float32),
        ],
        scratch_shapes=[
            pltpu.VMEM((total * ROWS, width), jnp.bfloat16),
            pltpu.VMEM((total * ROWS, width), jnp.bfloat16),
            pltpu.VMEM((new * ROWS, total * ROWS), jnp.float32),
            pltpu.VMEM((max(old, 1) * ROWS, new * ROWS), jnp.float32),
            pltpu.VMEM((4, ROWS), jnp.float32),
            pltpu.SemaphoreType.DMA((total,)),
            pltpu.SemaphoreType.DMA((total,)),
            pltpu.SemaphoreType.DMA((total,)),
        ],
        input_output_aliases={3: 0} if before else {},
        compiler_params=pltpu.CompilerParams(vmem_limit_bytes=VMEM),
        cost_estimate=pl.CostEstimate(
            flops=2 * tiles * ROWS * ROWS * width,
            bytes_accessed=4 * tiles * ROWS * ROWS,
            transcendentals=tiles * ROWS * ROWS,
        ),
        name=name,
    )(table, scale, *before, *own, *other)


def join_kernel(shift, stats_ref, out_ref):
    rows = out_ref.shape[1] - 256
    peak = functools.reduce(jnp.maximum, [stats_ref[k, 0:1, :] for k in range(8)])
    total = weighted = matched = 0.0
    for k in range(8):
        shrink = jnp.exp2(stats_ref[k, 0:1, :] - peak)
        total = total + stats_ref[k, 1:2, :] * shrink
        weighted = weighted + stats_ref[k, 2:3, :] * shrink
        matched = matched + stats_ref[k, 3:4, :]
    lse = peak + jnp.log2(total)
    out_ref[:, :rows] = lse + shift
    for k, value in enumerate((lse - matched, weighted / total - matched)):
        value = jnp.sum(value, axis=1, keepdims=True)
        out_ref[:, rows + 128 * k : rows + 128 * (k + 1)] = jnp.broadcast_to(value, (1, 128))


def join_call(shift, stats):
    return pl.pallas_call(
        functools.partial(join_kernel, shift),
        out_shape=jax.ShapeDtypeStruct((1, stats.shape[2] + 256), jnp.float32),
        name="join",
    )(stats)


def grad_kernel(pairs, pieces, table_ref, scale_ref, own_lse_ref, other_lse_ref, scores_ref, *refs):
    count = len(pieces)
    other_refs, outs = refs[:8], refs[8 : 8 + count]
    weights, (blocks, own, other, out_sems, other_sem) = refs[8 + count : 8 + count + PAIR], refs[8 + count + PAIR :]
    step = pl.program_id(0)
    m = scores_ref.shape[1]
    load_other = fetch(other_refs, other, other_sem)
    stores = [
        pltpu.make_async_copy(own if q == 0 else blocks.at[k], outs[k], out_sems.at[k])
        for k, q in enumerate(pieces)
    ]

    @pl.when(step == 0)
    def _():
        for copy in load_other:
            copy.start()

    extra = other_lse_ref[:, m : m + 256]
    high = extra.astype(jnp.bfloat16).astype(jnp.float32)
    middle = (extra - high).astype(jnp.bfloat16).astype(jnp.float32)
    row = lax.broadcasted_iota(jnp.int32, (EXTRA, 256), 0)
    rows = [jnp.broadcast_to(v, (EXTRA, 256)) for v in (high, middle, extra - high - middle)]
    tile = jnp.where(row == 0, rows[0], jnp.where(row == 1, rows[1], jnp.where(row == 2, rows[2], 0.0)))
    ones = eye(128).astype(jnp.float32)

    def weigh(k):
        piece = pieces[k] - PAIR * step
        own_lse = to_column(own_lse_ref[:, pl.ds(table_place(table_ref, 0, piece), ROWS)])
        at_row = (PAIR - 1 - k) * ROWS
        found = [table_ref[piece * (ROWS // 128) + half] for half in range(ROWS // 128)]
        for at in range(0, m, ROWS):
            part = scores_ref[at_row : at_row + ROWS, at : at + ROWS]
            other_lse = other_lse_ref[:, pl.ds(table_place(table_ref, 1, at // ROWS), ROWS)]
            weight = jnp.exp2(part - own_lse) + jnp.exp2(part - other_lse)
            for i in range(0, ROWS, 128):
                for j in range(0, ROWS, 128):
                    taken = jnp.where(found[i // 128] == (at + j) // 128, 1.0 / pairs, 0.0)
                    weights[k][i : i + 128, at + j : at + j + 128] = (
                        weight[i : i + 128, j : j + 128] - ones * taken
                    ).astype(jnp.bfloat16)

    def multiply(k):
        grad = scale_ref[0] * jnp.dot(weights[k][...], other[...], preferred_element_type=jnp.float32)
        slot = PAIR * step + k
        blocks[slot, 0:ROWS, :] = grad.astype(jnp.bfloat16)
        blocks[slot, ROWS:, :] = jnp.zeros((EXTRA, blocks.shape[2]), jnp.bfloat16)
        blocks[slot, ROWS:, 0:256] = tile.astype(jnp.bfloat16)
        if pieces[-1] == 0 and k == PAIR - 1:
            own[...] = grad

    weigh(0)

    @pl.when(step == 0)
    def _():
        for copy in load_other:
            copy.wait()

    multiply(0)
    for k in range(1, PAIR):
        weigh(k)
        multiply(k)
    for at in range(0, count, PAIR):

        @pl.when(step == at // PAIR)
        def _():
            for k in range(at, at + PAIR):
                stores[k].start()

    @pl.when(step == count // PAIR - 1)
    def _():
        for store in stores:
            store.wait()


def grad_call(name, pairs, pieces, table, scale, scores, own_lse, other_lse, other):
    width = other[0].shape[1]
    count = len(pieces)
    m = scores.shape[1]
    smem, vmem, anywhere = (pl.BlockSpec(memory_space=s) for s in (pltpu.SMEM, pltpu.VMEM, pl.ANY))
    sent = jax.ShapeDtypeStruct((ROWS + EXTRA, width), jnp.bfloat16)
    kept = jax.ShapeDtypeStruct((ROWS, width), jnp.float32)
    return pl.pallas_call(
        functools.partial(grad_kernel, pairs, pieces),
        grid=(count // PAIR,),
        in_specs=[
            smem,
            smem,
            vmem,
            vmem,
            pl.BlockSpec((PAIR * ROWS, m), lambda i: (pieces[0] // PAIR - i, 0)),
        ]
        + [anywhere] * 8,
        out_specs=[anywhere] * count,
        out_shape=[kept if q == 0 else sent for q in pieces],
        scratch_shapes=[pltpu.VMEM((ROWS, m), jnp.bfloat16)] * PAIR
        + [
            pltpu.VMEM((count, ROWS + EXTRA, width), jnp.bfloat16),
            pltpu.VMEM((ROWS, width), jnp.float32),
            pltpu.VMEM((m, width), jnp.bfloat16),
            pltpu.SemaphoreType.DMA((count,)),
            pltpu.SemaphoreType.DMA((8,)),
        ],
        compiler_params=pltpu.CompilerParams(vmem_limit_bytes=VMEM),
        cost_estimate=pl.CostEstimate(
            flops=2 * count * ROWS * m * width,
            bytes_accessed=4 * count * ROWS * m,
            transcendentals=2 * count * ROWS * m,
        ),
        name=name,
    )(table, scale, own_lse, other_lse, scores, *other)


def on_device(images, texts, logit_scale):
    shard, width = images.shape
    pairs = shard * 128
    me = lax.axis_index(AXES)
    first = lax.rem(lax.axis_index("row"), 2) == 0
    swap = functools.partial(lax.ppermute, axis_name=AXES, perm=partner_perm())
    members = [list(g) for g in groups()]
    table = lax.dynamic_slice(jnp.asarray(tables()), (me, 0), (1, 32)).reshape(-1)
    scale2 = (logit_scale * LOG2E).reshape(1)

    def send(value, steps, pair):
        return lax.ppermute(value, AXES, ring_perm(steps, pair))

    got = swap(jnp.where(first, texts, images))
    mine = jnp.where(first, images, texts)
    chip = jnp.concatenate([jnp.where(first, mine, got), jnp.where(first, got, mine)], axis=0)

    after, before, across = send(chip, -1, 0), send(chip, 1, 0), send(chip, 0, 1)
    own = [chip, after, before, across]
    middle = [send(after, -1, 0), send(across, 1, 0), send(after, 0, 1)]
    other = [swap(v) for v in own]
    scores, stats = score_call("scores_near", False, table, scale2, (), own, other)
    stats, *middle = lax.optimization_barrier((stats, *middle))
    far = send(middle[2], -1, 0)
    own, other = own + middle, other + [swap(v) for v in middle]
    scores, stats = score_call("scores_middle", False, table, scale2, (stats, scores), own, other)
    stats, far = lax.optimization_barrier((stats, far))
    own, other = own + [far], other + [swap(far)]
    scores, stats = score_call("scores_far", True, table, scale2, (stats, scores), own, other)

    spread = lax.all_to_all(stats, AXES, 0, 0, axis_index_groups=members, tiled=True)
    own_lse = join_call(float(np.log2(2.0 * pairs)), spread)
    other_lse = swap(own_lse)

    def grads(name, pieces):
        return grad_call(name, pairs, pieces, table, logit_scale.reshape(1), scores, own_lse, other_lse, other)

    received = [send(v, *PIECES[q]) for q, v in zip((7, 6, 5, 4), grads("grads_far", (7, 6, 5, 4)))]
    *near_grads, kept = grads("grads_near", (3, 2, 1, 0))
    received[0], near_grads = lax.optimization_barrier((received[0], near_grads))
    received += [send(v, *PIECES[q]) for q, v in zip((3, 2, 1), near_grads)]
    received = [v.astype(jnp.float32) for v in received]
    summed = functools.reduce(jnp.add, [v[:ROWS] for v in received]) + kept
    parts = functools.reduce(jnp.add, [jnp.sum(v[ROWS : ROWS + 3, 0:256], axis=0, keepdims=True) for v in received])
    parts = parts + other_lse[:, 16 * shard :]
    parts = jnp.pad(parts, ((0, 7), (0, width - 256)))
    keep = jnp.where(first, summed[:shard], summed[shard:])
    back = swap(jnp.concatenate([jnp.where(first, summed[shard:], summed[:shard]), parts], axis=0))
    parts = (parts[0] + back[shard]) * (LN2 / (2.0 * pairs))
    return (
        parts[0],
        jnp.where(first, keep, back[:shard]),
        jnp.where(first, back[:shard], keep),
        parts[128] / logit_scale,
    )


def solution(mesh):
    in_specs = (P(("row", "col"), None), P(("col", "row"), None), P())
    out_specs = (P(), P(("row", "col"), None), P(("col", "row"), None), P())
    return jax.shard_map(
        on_device, mesh=mesh, in_specs=in_specs, out_specs=out_specs, check_vma=False
    )
```

```python
import functools
import itertools

import jax
import jax.numpy as jnp
import numpy as np
from jax import lax
from jax.experimental import pallas as pl
from jax.experimental.pallas import tpu as pltpu
from jax.sharding import PartitionSpec as P

LOG2E = 1.4426950408889634
LN2 = 0.6931471805599453
AXES = ("row", "col")
ROWS = 256
VMEM = 24 * 1024 * 1024
GRAD_VMEM = 63_400_000
SPARE = 3328
EXTRA = 16
PAIR = 2


def linear(x, y, z, core):
    return (((x % 2) * 2 + core) * 4 + z) * 8 + (x // 2) * 4 + y


def devices():
    return itertools.product(range(4), range(4), range(4), range(2))


def partner_perm():
    return [(linear(x, y, z, c), linear(x, y, z, 1 - c)) for x, y, z, c in devices()]


PIECES = ((0, 0), (1, 0), (-1, 0), (0, 1), (2, 0), (-1, 1), (1, 1), (2, 1))


def moved(x, y, z, core, steps, pair):
    if core == 0:
        return (3 - x if pair else x, (y + steps) % 4, z, core)
    return (x ^ 1 if pair else x, y, (z + steps) % 4, core)


def ring_perm(steps, pair):
    return [(linear(*d), linear(*moved(*d, steps, pair))) for d in devices()]


def group_of(x, y, z, core):
    return sorted(linear(*moved(x, y, z, core, steps, pair)) for steps, pair in PIECES)


def groups():
    return sorted(set(tuple(group_of(*d)) for d in devices()))


def block_ids(x, y, z, core):
    out = []
    for steps, pair in PIECES:
        member = linear(*moved(x, y, z, core, steps, pair))
        row, col = member // 32, member % 32
        for c in (0, 1):
            at = (row // 2) * 2 + c
            out.append(at * 32 + col if core == 0 else col * 4 + at)
    return out


def tables():
    table = np.full((128, 32), -1, np.int32)
    for d in devices():
        x, y, z, c = d
        own, other = block_ids(x, y, z, c), block_ids(x, y, z, 1 - c)
        for k, block in enumerate(own):
            if block in other:
                table[linear(*d), k] = other.index(block)
        for side in (0, 1):
            e = (x, y, z, c ^ side)
            for k, (steps, pair) in enumerate(PIECES):
                table[linear(*d), 16 + 8 * side + k] = group_of(*e).index(linear(*moved(*e, steps, pair)))
    return table


def to_column(row):
    n = row.shape[1]
    eye = lax.broadcasted_iota(jnp.int32, (n, n), 0) == lax.broadcasted_iota(jnp.int32, (n, n), 1)
    return jnp.sum(jnp.where(eye, jnp.broadcast_to(row, (n, n)), 0.0), axis=1, keepdims=True)


def eye(n):
    return lax.broadcasted_iota(jnp.int32, (n, n), 0) == lax.broadcasted_iota(jnp.int32, (n, n), 1)


def fetch(parts, whole, sems):
    return [
        pltpu.make_async_copy(part, whole.at[pl.ds(k * ROWS, ROWS)], sems.at[k]) for k, part in enumerate(parts)
    ]


def table_place(table_ref, side, piece):
    return pl.multiple_of(table_ref[16 + 8 * side + piece] * ROWS, ROWS)


def tile_stats(scale, rows, other_at, width, scores_ref):
    chunk = 512 if width % 512 == 0 else 256
    peak = total = weighted = None
    for at in range(0, width, chunk):
        scores = scale * lax.dot_general(
            rows, other_at(at, chunk), (((1,), (1,)), ((), ())), preferred_element_type=jnp.float32
        )
        scores_ref[:, at : at + chunk] = scores
        parts = [scores[:, k : k + 128] for k in range(0, chunk, 128)]
        top = functools.reduce(jnp.maximum, parts)
        if peak is not None:
            top = jnp.maximum(top, peak)
        powers = [jnp.exp2(part - top) for part in parts]
        new_total = functools.reduce(jnp.add, powers)
        new_weighted = functools.reduce(jnp.add, [a * b for a, b in zip(powers, parts)])
        if peak is not None:
            shrink = jnp.exp2(peak - top)
            new_total = new_total + total * shrink
            new_weighted = new_weighted + weighted * shrink
        peak, total, weighted = top, new_total, new_weighted
    peak = peak.T
    top = jnp.max(peak, axis=0, keepdims=True)
    shrink = jnp.exp2(peak - top)
    return (
        top,
        jnp.sum(total.T * shrink, axis=0, keepdims=True),
        jnp.sum(weighted.T * shrink, axis=0, keepdims=True),
    )


def put_matched(table_ref, piece, begin, width, scores_ref, line):
    line[3:4, :] = jnp.zeros((1, ROWS), jnp.float32)
    for half in range(ROWS // 128):
        place = table_ref[piece * (ROWS // 128) + half] * 128 - begin

        @pl.when(jnp.logical_and(place >= 0, place < width))
        def _():
            span = slice(half * 128, half * 128 + 128)
            corner = scores_ref[span, pl.ds(pl.multiple_of(place, 128), 128)]
            line[3:4, span] = jnp.sum(jnp.where(eye(128), corner, 0.0), axis=0, keepdims=True)


def score_kernel(old, new, last, table_ref, scale_ref, *refs):
    total = old + new
    if old:
        before_ref, refs = refs[0], refs[2:]
    own_refs, other_refs = refs[:total], refs[total : 2 * total]
    scores_out, stats_ref, own, other, row, column, line, own_sems, other_sems, out_sems = refs[2 * total :]
    load_own, load_other = fetch(own_refs, own, own_sems), fetch(other_refs, other, other_sems)
    for copy in load_own[old:] + load_other + load_own[:old]:
        copy.start()

    def piece_rows(k):
        return pl.ds(k * ROWS if isinstance(k, int) else pl.multiple_of(k * ROWS, ROWS), ROWS)

    def store_old(k):
        return pltpu.make_async_copy(
            column.at[piece_rows(k)],
            scores_out.at[piece_rows(k), pl.ds(old * ROWS, new * ROWS)],
            out_sems.at[k],
        )

    def store_new(k):
        return pltpu.make_async_copy(
            row.at[piece_rows(k)],
            scores_out.at[piece_rows(k + old), pl.ds(0, total * ROWS)],
            out_sems.at[k + old],
        )

    def put(piece, top, power, weighted):
        line[0:1, :] = top
        line[1:2, :] = power
        line[2:3, :] = weighted
        if last:
            for member in range(8):
                stats_ref[member, :, pl.ds(table_place(table_ref, 0, piece), ROWS)] = line[...]
        else:
            stats_ref[:, piece_rows(piece)] = line[...]

    def part(at, size):
        if new == 1:
            for k in range(at // ROWS, (at + size) // ROWS):
                load_other[k].wait()
        return other[at : at + size, :]

    def new_piece(k):
        target = row.at[piece_rows(k)]
        top, power, weighted = tile_stats(scale_ref[0], own[piece_rows(k + old), :], part, total * ROWS, target)
        store_new(k).start()
        put_matched(table_ref, k + old, 0, total * ROWS, target, line)
        put(k + old, top, power, weighted)

    def old_scores(k):
        stats = tile_stats(
            scale_ref[0],
            own[piece_rows(k), :],
            lambda at, size: other[old * ROWS + at : old * ROWS + at + size, :],
            new * ROWS,
            column.at[piece_rows(k)],
        )
        store_old(k).start()
        return stats

    def old_stats(k, top, power, weighted):
        put_matched(table_ref, k, old * ROWS, new * ROWS, column.at[piece_rows(k)], line)
        earlier = before_ref[:, piece_rows(k)]
        new_top = jnp.maximum(earlier[0:1], top)
        old_shrink, new_shrink = jnp.exp2(earlier[0:1] - new_top), jnp.exp2(top - new_top)
        line[3:4, :] = earlier[3:4] + line[3:4, :]
        put(k, new_top, earlier[1:2] * old_shrink + power * new_shrink, earlier[2:3] * old_shrink + weighted * new_shrink)

    for copy in load_own[old:] + (load_other if new > 1 else []):
        copy.wait()
    if new == 1:
        new_piece(0)
    else:
        pl.loop(0, new)(new_piece)
    for copy in load_own[:old]:
        copy.wait()
    if new == 1:
        found = [old_scores(k) for k in range(old)]
        for k, stats in enumerate(found):
            old_stats(k, *stats)
    elif old:
        pl.loop(0, old)(lambda k: old_stats(k, *old_scores(k)))
    for k in range(old):
        store_old(k).wait()
    for k in range(new):
        store_new(k).wait()


def score_call(name, last, table, scale, before, own, other):
    total, width = len(own), own[0].shape[1]
    old = before[0].shape[1] // ROWS if before else 0
    new = total - old
    smem, vmem, anywhere = (pl.BlockSpec(memory_space=s) for s in (pltpu.SMEM, pltpu.VMEM, pl.ANY))
    tiles = new * total + old * new
    return pl.pallas_call(
        functools.partial(score_kernel, old, new, last),
        in_specs=[smem, smem] + ([vmem, anywhere] if before else []) + [anywhere] * (2 * total),
        out_specs=[anywhere, vmem],
        out_shape=[
            jax.ShapeDtypeStruct((8 * ROWS + SPARE, 8 * ROWS), jnp.float32),
            jax.ShapeDtypeStruct((8, 4, total * ROWS) if last else (4, total * ROWS), jnp.float32),
        ],
        scratch_shapes=[
            pltpu.VMEM((total * ROWS, width), jnp.bfloat16),
            pltpu.VMEM((total * ROWS, width), jnp.bfloat16),
            pltpu.VMEM((new * ROWS, total * ROWS), jnp.float32),
            pltpu.VMEM((max(old, 1) * ROWS, new * ROWS), jnp.float32),
            pltpu.VMEM((4, ROWS), jnp.float32),
            pltpu.SemaphoreType.DMA((total,)),
            pltpu.SemaphoreType.DMA((total,)),
            pltpu.SemaphoreType.DMA((total,)),
        ],
        input_output_aliases={3: 0} if before else {},
        compiler_params=pltpu.CompilerParams(vmem_limit_bytes=VMEM),
        cost_estimate=pl.CostEstimate(
            flops=2 * tiles * ROWS * ROWS * width,
            bytes_accessed=4 * tiles * ROWS * ROWS,
            transcendentals=tiles * ROWS * ROWS,
        ),
        name=name,
    )(table, scale, *before, *own, *other)


def join_kernel(shift, stats_ref, out_ref):
    rows = out_ref.shape[1] - 256
    peak = functools.reduce(jnp.maximum, [stats_ref[k, 0:1, :] for k in range(8)])
    total = weighted = matched = 0.0
    for k in range(8):
        shrink = jnp.exp2(stats_ref[k, 0:1, :] - peak)
        total = total + stats_ref[k, 1:2, :] * shrink
        weighted = weighted + stats_ref[k, 2:3, :] * shrink
        matched = matched + stats_ref[k, 3:4, :]
    lse = peak + jnp.log2(total)
    out_ref[:, :rows] = lse + shift
    for k, value in enumerate((lse - matched, weighted / total - matched)):
        value = jnp.sum(value, axis=1, keepdims=True)
        out_ref[:, rows + 128 * k : rows + 128 * (k + 1)] = jnp.broadcast_to(value, (1, 128))


def join_call(shift, stats):
    return pl.pallas_call(
        functools.partial(join_kernel, shift),
        out_shape=jax.ShapeDtypeStruct((1, stats.shape[2] + 256), jnp.float32),
        name="join",
    )(stats)


def grad_kernel(pairs, pieces, table_ref, scale_ref, own_lse_ref, other_lse_ref, scores_ref, *refs):
    count = len(pieces)
    other_refs, outs = refs[:8], refs[8 : 8 + count]
    weights, (blocks, own, other, out_sems, other_sem) = refs[8 + count : 8 + count + PAIR], refs[8 + count + PAIR :]
    step = pl.program_id(0)
    m = scores_ref.shape[1]
    load_other = fetch(other_refs, other, other_sem)
    stores = [
        pltpu.make_async_copy(own if q == 0 else blocks.at[k], outs[k], out_sems.at[k])
        for k, q in enumerate(pieces)
    ]

    @pl.when(step == 0)
    def _():
        for copy in load_other:
            copy.start()

    extra = other_lse_ref[:, m : m + 256]
    high = extra.astype(jnp.bfloat16).astype(jnp.float32)
    middle = (extra - high).astype(jnp.bfloat16).astype(jnp.float32)
    row = lax.broadcasted_iota(jnp.int32, (EXTRA, 256), 0)
    rows = [jnp.broadcast_to(v, (EXTRA, 256)) for v in (high, middle, extra - high - middle)]
    tile = jnp.where(row == 0, rows[0], jnp.where(row == 1, rows[1], jnp.where(row == 2, rows[2], 0.0)))
    ones = eye(128).astype(jnp.float32)

    def weigh(k):
        piece = pieces[k] - PAIR * step
        own_lse = to_column(own_lse_ref[:, pl.ds(table_place(table_ref, 0, piece), ROWS)])
        at_row = (PAIR - 1 - k) * ROWS
        found = [table_ref[piece * (ROWS // 128) + half] for half in range(ROWS // 128)]
        for at in range(0, m, ROWS):
            part = scores_ref[at_row : at_row + ROWS, at : at + ROWS]
            other_lse = other_lse_ref[:, pl.ds(table_place(table_ref, 1, at // ROWS), ROWS)]
            weight = jnp.exp2(part - own_lse) + jnp.exp2(part - other_lse)
            for i in range(0, ROWS, 128):
                for j in range(0, ROWS, 128):
                    taken = jnp.where(found[i // 128] == (at + j) // 128, 1.0 / pairs, 0.0)
                    weights[k][i : i + 128, at + j : at + j + 128] = (
                        weight[i : i + 128, j : j + 128] - ones * taken
                    ).astype(jnp.bfloat16)

    def multiply(k):
        grad = scale_ref[0] * jnp.dot(weights[k][...], other[...], preferred_element_type=jnp.float32)
        slot = PAIR * step + k
        blocks[slot, 0:ROWS, :] = grad.astype(jnp.bfloat16)
        blocks[slot, ROWS:, :] = jnp.zeros((EXTRA, blocks.shape[2]), jnp.bfloat16)
        blocks[slot, ROWS:, 0:256] = tile.astype(jnp.bfloat16)
        if pieces[-1] == 0 and k == PAIR - 1:
            own[...] = grad

    weigh(0)

    @pl.when(step == 0)
    def _():
        for copy in load_other:
            copy.wait()

    multiply(0)
    for k in range(1, PAIR):
        weigh(k)
        multiply(k)
    for at in range(0, count, PAIR):

        @pl.when(step == at // PAIR)
        def _():
            for k in range(at, at + PAIR):
                stores[k].start()

    @pl.when(step == count // PAIR - 1)
    def _():
        for store in stores:
            store.wait()


def grad_call(name, pairs, pieces, table, scale, scores, own_lse, other_lse, other):
    width = other[0].shape[1]
    count = len(pieces)
    m = scores.shape[1]
    smem, vmem, anywhere = (pl.BlockSpec(memory_space=s) for s in (pltpu.SMEM, pltpu.VMEM, pl.ANY))
    sent = jax.ShapeDtypeStruct((ROWS + EXTRA, width), jnp.bfloat16)
    kept = jax.ShapeDtypeStruct((ROWS, width), jnp.float32)
    return pl.pallas_call(
        functools.partial(grad_kernel, pairs, pieces),
        grid=(count // PAIR,),
        in_specs=[
            smem,
            smem,
            vmem,
            vmem,
            pl.BlockSpec((PAIR * ROWS, m), lambda i: (pieces[0] // PAIR - i, 0)),
        ]
        + [anywhere] * 8,
        out_specs=[anywhere] * count,
        out_shape=[kept if q == 0 else sent for q in pieces],
        scratch_shapes=[pltpu.VMEM((ROWS, m), jnp.bfloat16)] * PAIR
        + [
            pltpu.VMEM((count, ROWS + EXTRA, width), jnp.bfloat16),
            pltpu.VMEM((ROWS, width), jnp.float32),
            pltpu.VMEM((m, width), jnp.bfloat16),
            pltpu.SemaphoreType.DMA((count,)),
            pltpu.SemaphoreType.DMA((8,)),
        ],
        compiler_params=pltpu.CompilerParams(vmem_limit_bytes=GRAD_VMEM),
        cost_estimate=pl.CostEstimate(
            flops=2 * count * ROWS * m * width,
            bytes_accessed=4 * count * ROWS * m,
            transcendentals=2 * count * ROWS * m,
        ),
        name=name,
    )(table, scale, own_lse, other_lse, scores, *other)


def on_device(images, texts, logit_scale):
    shard, width = images.shape
    pairs = shard * 128
    me = lax.axis_index(AXES)
    first = lax.rem(lax.axis_index("row"), 2) == 0
    swap = functools.partial(lax.ppermute, axis_name=AXES, perm=partner_perm())
    members = [list(g) for g in groups()]
    table = lax.dynamic_slice(jnp.asarray(tables()), (me, 0), (1, 32)).reshape(-1)
    scale2 = (logit_scale * LOG2E).reshape(1)

    def send(value, steps, pair):
        return lax.ppermute(value, AXES, ring_perm(steps, pair))

    got = swap(jnp.where(first, texts, images))
    mine = jnp.where(first, images, texts)
    chip = jnp.concatenate([jnp.where(first, mine, got), jnp.where(first, got, mine)], axis=0)

    after, before, across = send(chip, -1, 0), send(chip, 1, 0), send(chip, 0, 1)
    own = [chip, after, before, across]
    middle = [send(after, -1, 0), send(across, 1, 0), send(after, 0, 1)]
    other = [swap(v) for v in own]
    scores, stats = score_call("scores_near", False, table, scale2, (), own, other)
    stats, *middle = lax.optimization_barrier((stats, *middle))
    far = send(middle[2], -1, 0)
    own, other = own + middle, other + [swap(v) for v in middle]
    scores, stats = score_call("scores_middle", False, table, scale2, (stats, scores), own, other)
    stats, far = lax.optimization_barrier((stats, far))
    own, other = own + [far], other + [swap(far)]
    scores, stats = score_call("scores_far", True, table, scale2, (stats, scores), own, other)

    spread = lax.all_to_all(stats, AXES, 0, 0, axis_index_groups=members, tiled=True)
    own_lse = join_call(float(np.log2(2.0 * pairs)), spread)
    other_lse = swap(own_lse)

    def grads(name, pieces):
        return grad_call(name, pairs, pieces, table, logit_scale.reshape(1), scores, own_lse, other_lse, other)

    received = [send(v, *PIECES[q]) for q, v in zip((7, 6, 5, 4), grads("grads_far", (7, 6, 5, 4)))]
    *near_grads, kept = grads("grads_near", (3, 2, 1, 0))
    received[0], near_grads = lax.optimization_barrier((received[0], near_grads))
    received += [send(v, *PIECES[q]) for q, v in zip((3, 2, 1), near_grads)]
    received = [v.astype(jnp.float32) for v in received]
    summed = functools.reduce(jnp.add, [v[:ROWS] for v in received]) + kept
    parts = functools.reduce(jnp.add, [jnp.sum(v[ROWS : ROWS + 3, 0:256], axis=0, keepdims=True) for v in received])
    parts = parts + other_lse[:, 16 * shard :]
    parts = jnp.pad(parts, ((0, 7), (0, width - 256)))
    keep = jnp.where(first, summed[:shard], summed[shard:])
    back = swap(jnp.concatenate([jnp.where(first, summed[shard:], summed[:shard]), parts], axis=0))
    parts = (parts[0] + back[shard]) * (LN2 / (2.0 * pairs))
    return (
        parts[0],
        jnp.where(first, keep, back[:shard]),
        jnp.where(first, back[:shard], keep),
        parts[128] / logit_scale,
    )


def solution(mesh):
    in_specs = (P(("row", "col"), None), P(("col", "row"), None), P())
    out_specs = (P(), P(("row", "col"), None), P(("col", "row"), None), P())
    return jax.shard_map(
        on_device, mesh=mesh, in_specs=in_specs, out_specs=out_specs, check_vma=False
    )
```

```python
import functools
import itertools

import jax
import jax.numpy as jnp
import numpy as np
from jax import lax
from jax.experimental import pallas as pl
from jax.experimental.pallas import tpu as pltpu
from jax.sharding import PartitionSpec as P

LOG2E = 1.4426950408889634
LN2 = 0.6931471805599453
AXES = ("row", "col")
ROWS = 256
VMEM = 24 * 1024 * 1024
GRAD_VMEM = 63_400_000
SPARE = 3328
EXTRA = 16
PAIR = 2


def linear(x, y, z, core):
    return (((x % 2) * 2 + core) * 4 + z) * 8 + (x // 2) * 4 + y


def devices():
    return itertools.product(range(4), range(4), range(4), range(2))


def partner_perm():
    return [(linear(x, y, z, c), linear(x, y, z, 1 - c)) for x, y, z, c in devices()]


PIECES = ((0, 0), (1, 0), (-1, 0), (0, 1), (2, 0), (-1, 1), (1, 1), (2, 1))


def moved(x, y, z, core, steps, pair):
    if core == 0:
        return (3 - x if pair else x, (y + steps) % 4, z, core)
    return (x ^ 1 if pair else x, y, (z + steps) % 4, core)


def ring_perm(steps, pair):
    return [(linear(*d), linear(*moved(*d, steps, pair))) for d in devices()]


def group_of(x, y, z, core):
    return sorted(linear(*moved(x, y, z, core, steps, pair)) for steps, pair in PIECES)


def groups():
    return sorted(set(tuple(group_of(*d)) for d in devices()))


def block_ids(x, y, z, core):
    out = []
    for steps, pair in PIECES:
        member = linear(*moved(x, y, z, core, steps, pair))
        row, col = member // 32, member % 32
        for c in (0, 1):
            at = (row // 2) * 2 + c
            out.append(at * 32 + col if core == 0 else col * 4 + at)
    return out


def tables():
    table = np.full((128, 32), -1, np.int32)
    for d in devices():
        x, y, z, c = d
        own, other = block_ids(x, y, z, c), block_ids(x, y, z, 1 - c)
        for k, block in enumerate(own):
            if block in other:
                table[linear(*d), k] = other.index(block)
        for side in (0, 1):
            e = (x, y, z, c ^ side)
            for k, (steps, pair) in enumerate(PIECES):
                table[linear(*d), 16 + 8 * side + k] = group_of(*e).index(linear(*moved(*e, steps, pair)))
    return table


def to_column(row):
    n = row.shape[1]
    eye = lax.broadcasted_iota(jnp.int32, (n, n), 0) == lax.broadcasted_iota(jnp.int32, (n, n), 1)
    return jnp.sum(jnp.where(eye, jnp.broadcast_to(row, (n, n)), 0.0), axis=1, keepdims=True)


def eye(n):
    return lax.broadcasted_iota(jnp.int32, (n, n), 0) == lax.broadcasted_iota(jnp.int32, (n, n), 1)


def fetch(parts, whole, sems):
    return [
        pltpu.make_async_copy(part, whole.at[pl.ds(k * ROWS, ROWS)], sems.at[k]) for k, part in enumerate(parts)
    ]


def table_place(table_ref, side, piece):
    return pl.multiple_of(table_ref[16 + 8 * side + piece] * ROWS, ROWS)


def tile_stats(scale, rows, other_at, width, scores_ref):
    chunk = 512 if width % 512 == 0 else 256
    peak = total = weighted = None
    for at in range(0, width, chunk):
        scores = scale * lax.dot_general(
            rows, other_at(at, chunk), (((1,), (1,)), ((), ())), preferred_element_type=jnp.float32
        )
        scores_ref[:, at : at + chunk] = scores
        parts = [scores[:, k : k + 128] for k in range(0, chunk, 128)]
        top = functools.reduce(jnp.maximum, parts)
        if peak is not None:
            top = jnp.maximum(top, peak)
        powers = [jnp.exp2(part - top) for part in parts]
        new_total = functools.reduce(jnp.add, powers)
        new_weighted = functools.reduce(jnp.add, [a * b for a, b in zip(powers, parts)])
        if peak is not None:
            shrink = jnp.exp2(peak - top)
            new_total = new_total + total * shrink
            new_weighted = new_weighted + weighted * shrink
        peak, total, weighted = top, new_total, new_weighted
    peak = peak.T
    top = jnp.max(peak, axis=0, keepdims=True)
    shrink = jnp.exp2(peak - top)
    return (
        top,
        jnp.sum(total.T * shrink, axis=0, keepdims=True),
        jnp.sum(weighted.T * shrink, axis=0, keepdims=True),
    )


def put_matched(table_ref, piece, begin, width, scores_ref, line):
    line[3:4, :] = jnp.zeros((1, ROWS), jnp.float32)
    for half in range(ROWS // 128):
        place = table_ref[piece * (ROWS // 128) + half] * 128 - begin

        @pl.when(jnp.logical_and(place >= 0, place < width))
        def _():
            span = slice(half * 128, half * 128 + 128)
            corner = scores_ref[span, pl.ds(pl.multiple_of(place, 128), 128)]
            line[3:4, span] = jnp.sum(jnp.where(eye(128), corner, 0.0), axis=0, keepdims=True)


def score_kernel(old, new, last, table_ref, scale_ref, *refs):
    total = old + new
    if old:
        before_ref, refs = refs[0], refs[2:]
    own_refs, other_refs = refs[:total], refs[total : 2 * total]
    scores_out, stats_ref, own, other, row, column, line, own_sems, other_sems, out_sems = refs[2 * total :]
    load_own, load_other = fetch(own_refs, own, own_sems), fetch(other_refs, other, other_sems)
    for copy in load_own[old:] + load_other + load_own[:old]:
        copy.start()

    def piece_rows(k):
        return pl.ds(k * ROWS if isinstance(k, int) else pl.multiple_of(k * ROWS, ROWS), ROWS)

    def store_old(k):
        return pltpu.make_async_copy(
            column.at[piece_rows(k)],
            scores_out.at[piece_rows(k), pl.ds(old * ROWS, new * ROWS)],
            out_sems.at[k],
        )

    def store_new(k):
        return pltpu.make_async_copy(
            row.at[piece_rows(k)],
            scores_out.at[piece_rows(k + old), pl.ds(0, total * ROWS)],
            out_sems.at[k + old],
        )

    def put(piece, top, power, weighted):
        line[0:1, :] = top
        line[1:2, :] = power
        line[2:3, :] = weighted
        if last:
            columns = pl.ds(table_place(table_ref, 0, piece), ROWS)
            lse, mean = top + jnp.log2(power), weighted / power
            line[4:5, :] += line[3:4, :]
            for member in range(8):
                stats_ref[member, 0:1, columns] = lse
                stats_ref[member, 1:2, columns] = mean
        else:
            stats_ref[:, piece_rows(piece)] = line[0:4, :]

    def part(at, size):
        if new == 1:
            for k in range(at // ROWS, (at + size) // ROWS):
                load_other[k].wait()
        return other[at : at + size, :]

    def new_piece(k):
        target = row.at[piece_rows(k)]
        top, power, weighted = tile_stats(scale_ref[0], own[piece_rows(k + old), :], part, total * ROWS, target)
        store_new(k).start()
        put_matched(table_ref, k + old, 0, total * ROWS, target, line)
        put(k + old, top, power, weighted)

    def old_scores(k):
        stats = tile_stats(
            scale_ref[0],
            own[piece_rows(k), :],
            lambda at, size: other[old * ROWS + at : old * ROWS + at + size, :],
            new * ROWS,
            column.at[piece_rows(k)],
        )
        store_old(k).start()
        return stats

    def old_stats(k, top, power, weighted):
        put_matched(table_ref, k, old * ROWS, new * ROWS, column.at[piece_rows(k)], line)
        earlier = before_ref[:, piece_rows(k)]
        new_top = jnp.maximum(earlier[0:1], top)
        old_shrink, new_shrink = jnp.exp2(earlier[0:1] - new_top), jnp.exp2(top - new_top)
        line[3:4, :] = earlier[3:4] + line[3:4, :]
        put(k, new_top, earlier[1:2] * old_shrink + power * new_shrink, earlier[2:3] * old_shrink + weighted * new_shrink)

    line[4:5, :] = jnp.zeros((1, ROWS), jnp.float32)
    for copy in load_own[old:] + (load_other if new > 1 else []):
        copy.wait()
    if new == 1:
        new_piece(0)
    else:
        pl.loop(0, new)(new_piece)
    for copy in load_own[:old]:
        copy.wait()
    if new == 1:
        found = [old_scores(k) for k in range(old)]
        for k, stats in enumerate(found):
            old_stats(k, *stats)
    elif old:
        pl.loop(0, old)(lambda k: old_stats(k, *old_scores(k)))
    for k in range(old):
        store_old(k).wait()
    if last:
        matched = jnp.broadcast_to(jnp.sum(line[4:5, :], axis=1, keepdims=True), (2, 128))
        for member in range(8):
            stats_ref[member, :, total * ROWS :] = matched
    for k in range(new):
        store_new(k).wait()


def score_call(name, last, table, scale, before, own, other):
    total, width = len(own), own[0].shape[1]
    old = before[0].shape[1] // ROWS if before else 0
    new = total - old
    smem, vmem, anywhere = (pl.BlockSpec(memory_space=s) for s in (pltpu.SMEM, pltpu.VMEM, pl.ANY))
    tiles = new * total + old * new
    return pl.pallas_call(
        functools.partial(score_kernel, old, new, last),
        in_specs=[smem, smem] + ([vmem, anywhere] if before else []) + [anywhere] * (2 * total),
        out_specs=[anywhere, vmem],
        out_shape=[
            jax.ShapeDtypeStruct((8 * ROWS + SPARE, 8 * ROWS), jnp.float32),
            jax.ShapeDtypeStruct((8, 2, total * ROWS + 128) if last else (4, total * ROWS), jnp.float32),
        ],
        scratch_shapes=[
            pltpu.VMEM((total * ROWS, width), jnp.bfloat16),
            pltpu.VMEM((total * ROWS, width), jnp.bfloat16),
            pltpu.VMEM((new * ROWS, total * ROWS), jnp.float32),
            pltpu.VMEM((max(old, 1) * ROWS, new * ROWS), jnp.float32),
            pltpu.VMEM((8, ROWS), jnp.float32),
            pltpu.SemaphoreType.DMA((total,)),
            pltpu.SemaphoreType.DMA((total,)),
            pltpu.SemaphoreType.DMA((total,)),
        ],
        input_output_aliases={3: 0} if before else {},
        compiler_params=pltpu.CompilerParams(vmem_limit_bytes=VMEM),
        cost_estimate=pl.CostEstimate(
            flops=2 * tiles * ROWS * ROWS * width,
            bytes_accessed=4 * tiles * ROWS * ROWS,
            transcendentals=tiles * ROWS * ROWS,
        ),
        name=name,
    )(table, scale, *before, *own, *other)


def join_kernel(shift, stats_ref, out_ref):
    rows = out_ref.shape[1] - 256
    peak = functools.reduce(jnp.maximum, [stats_ref[k, 0:1, :rows] for k in range(8)])
    total = weighted = matched = 0.0
    for k in range(8):
        power = jnp.exp2(stats_ref[k, 0:1, :rows] - peak)
        total = total + power
        weighted = weighted + stats_ref[k, 1:2, :rows] * power
        matched = matched + stats_ref[k, 0:1, rows:]
    lse = peak + jnp.log2(total)
    out_ref[:, :rows] = lse + shift
    for k, value in enumerate((lse, weighted / total)):
        value = jnp.sum(value, axis=1, keepdims=True)
        out_ref[:, rows + 128 * k : rows + 128 * (k + 1)] = jnp.broadcast_to(value, (1, 128)) - matched


def join_call(shift, stats):
    return pl.pallas_call(
        functools.partial(join_kernel, shift),
        out_shape=jax.ShapeDtypeStruct((1, stats.shape[2] + 128), jnp.float32),
        name="join",
    )(stats)


def grad_kernel(pairs, pieces, table_ref, scale_ref, own_lse_ref, other_lse_ref, scores_ref, *refs):
    count = len(pieces)
    other_refs, outs = refs[:8], refs[8 : 8 + count]
    weights, (blocks, own, other, out_sems, other_sem) = refs[8 + count : 8 + count + PAIR], refs[8 + count + PAIR :]
    step = pl.program_id(0)
    m = scores_ref.shape[1]
    load_other = fetch(other_refs, other, other_sem)
    stores = [
        pltpu.make_async_copy(own if q == 0 else blocks.at[k], outs[k], out_sems.at[k])
        for k, q in enumerate(pieces)
    ]

    @pl.when(step == 0)
    def _():
        for copy in load_other:
            copy.start()

    extra = other_lse_ref[:, m : m + 256]
    high = extra.astype(jnp.bfloat16).astype(jnp.float32)
    middle = (extra - high).astype(jnp.bfloat16).astype(jnp.float32)
    row = lax.broadcasted_iota(jnp.int32, (EXTRA, 256), 0)
    rows = [jnp.broadcast_to(v, (EXTRA, 256)) for v in (high, middle, extra - high - middle)]
    tile = jnp.where(row == 0, rows[0], jnp.where(row == 1, rows[1], jnp.where(row == 2, rows[2], 0.0)))
    ones = eye(128).astype(jnp.float32)

    def weigh(k):
        piece = pieces[k] - PAIR * step
        own_lse = to_column(own_lse_ref[:, pl.ds(table_place(table_ref, 0, piece), ROWS)])
        at_row = (PAIR - 1 - k) * ROWS
        found = [table_ref[piece * (ROWS // 128) + half] for half in range(ROWS // 128)]
        for at in range(0, m, ROWS):
            part = scores_ref[at_row : at_row + ROWS, at : at + ROWS]
            other_lse = other_lse_ref[:, pl.ds(table_place(table_ref, 1, at // ROWS), ROWS)]
            weight = jnp.exp2(part - own_lse) + jnp.exp2(part - other_lse)
            for i in range(0, ROWS, 128):
                for j in range(0, ROWS, 128):
                    taken = jnp.where(found[i // 128] == (at + j) // 128, 1.0 / pairs, 0.0)
                    weights[k][i : i + 128, at + j : at + j + 128] = (
                        weight[i : i + 128, j : j + 128] - ones * taken
                    ).astype(jnp.bfloat16)

    def multiply(k):
        grad = scale_ref[0] * jnp.dot(weights[k][...], other[...], preferred_element_type=jnp.float32)
        slot = PAIR * step + k
        blocks[slot, 0:ROWS, :] = grad.astype(jnp.bfloat16)
        blocks[slot, ROWS:, :] = jnp.zeros((EXTRA, blocks.shape[2]), jnp.bfloat16)
        blocks[slot, ROWS:, 0:256] = tile.astype(jnp.bfloat16)
        if pieces[-1] == 0 and k == PAIR - 1:
            own[...] = grad

    weigh(0)

    @pl.when(step == 0)
    def _():
        for copy in load_other:
            copy.wait()

    multiply(0)
    for k in range(1, PAIR):
        weigh(k)
        multiply(k)
    for at in range(0, count, PAIR):

        @pl.when(step == at // PAIR)
        def _():
            for k in range(at, at + PAIR):
                stores[k].start()

    @pl.when(step == count // PAIR - 1)
    def _():
        for store in stores:
            store.wait()


def grad_call(name, pairs, pieces, table, scale, scores, own_lse, other_lse, other):
    width = other[0].shape[1]
    count = len(pieces)
    m = scores.shape[1]
    smem, vmem, anywhere = (pl.BlockSpec(memory_space=s) for s in (pltpu.SMEM, pltpu.VMEM, pl.ANY))
    sent = jax.ShapeDtypeStruct((ROWS + EXTRA, width), jnp.bfloat16)
    kept = jax.ShapeDtypeStruct((ROWS, width), jnp.float32)
    return pl.pallas_call(
        functools.partial(grad_kernel, pairs, pieces),
        grid=(count // PAIR,),
        in_specs=[
            smem,
            smem,
            vmem,
            vmem,
            pl.BlockSpec((PAIR * ROWS, m), lambda i: (pieces[0] // PAIR - i, 0)),
        ]
        + [anywhere] * 8,
        out_specs=[anywhere] * count,
        out_shape=[kept if q == 0 else sent for q in pieces],
        scratch_shapes=[pltpu.VMEM((ROWS, m), jnp.bfloat16)] * PAIR
        + [
            pltpu.VMEM((count, ROWS + EXTRA, width), jnp.bfloat16),
            pltpu.VMEM((ROWS, width), jnp.float32),
            pltpu.VMEM((m, width), jnp.bfloat16),
            pltpu.SemaphoreType.DMA((count,)),
            pltpu.SemaphoreType.DMA((8,)),
        ],
        compiler_params=pltpu.CompilerParams(vmem_limit_bytes=GRAD_VMEM),
        cost_estimate=pl.CostEstimate(
            flops=2 * count * ROWS * m * width,
            bytes_accessed=4 * count * ROWS * m,
            transcendentals=2 * count * ROWS * m,
        ),
        name=name,
    )(table, scale, own_lse, other_lse, scores, *other)


def on_device(images, texts, logit_scale):
    shard, width = images.shape
    pairs = shard * 128
    me = lax.axis_index(AXES)
    first = lax.rem(lax.axis_index("row"), 2) == 0
    swap = functools.partial(lax.ppermute, axis_name=AXES, perm=partner_perm())
    members = [list(g) for g in groups()]
    table = lax.dynamic_slice(jnp.asarray(tables()), (me, 0), (1, 32)).reshape(-1)
    scale2 = (logit_scale * LOG2E).reshape(1)

    def send(value, steps, pair):
        return lax.ppermute(value, AXES, ring_perm(steps, pair))

    got = swap(jnp.where(first, texts, images))
    mine = jnp.where(first, images, texts)
    chip = jnp.concatenate([jnp.where(first, mine, got), jnp.where(first, got, mine)], axis=0)

    after, before, across = send(chip, -1, 0), send(chip, 1, 0), send(chip, 0, 1)
    own = [chip, after, before, across]
    middle = [send(after, -1, 0), send(across, 1, 0), send(after, 0, 1)]
    other = [swap(v) for v in own]
    scores, stats = score_call("scores_near", False, table, scale2, (), own, other)
    stats, *middle = lax.optimization_barrier((stats, *middle))
    far = send(middle[2], -1, 0)
    own, other = own + middle, other + [swap(v) for v in middle]
    scores, stats = score_call("scores_middle", False, table, scale2, (stats, scores), own, other)
    stats, far = lax.optimization_barrier((stats, far))
    own, other = own + [far], other + [swap(far)]
    scores, stats = score_call("scores_far", True, table, scale2, (stats, scores), own, other)

    spread = lax.all_to_all(stats, AXES, 0, 0, axis_index_groups=members, tiled=True)
    own_lse = join_call(float(np.log2(2.0 * pairs)), spread)
    other_lse = swap(own_lse)

    def grads(name, pieces):
        return grad_call(name, pairs, pieces, table, logit_scale.reshape(1), scores, own_lse, other_lse, other)

    received = [send(v, *PIECES[q]) for q, v in zip((7, 6, 5, 4), grads("grads_far", (7, 6, 5, 4)))]
    *near_grads, kept = grads("grads_near", (3, 2, 1, 0))
    received[0], near_grads = lax.optimization_barrier((received[0], near_grads))
    received += [send(v, *PIECES[q]) for q, v in zip((3, 2, 1), near_grads)]
    received = [v.astype(jnp.float32) for v in received]
    summed = functools.reduce(jnp.add, [v[:ROWS] for v in received]) + kept
    parts = functools.reduce(jnp.add, [jnp.sum(v[ROWS : ROWS + 3, 0:256], axis=0, keepdims=True) for v in received])
    parts = parts + other_lse[:, 16 * shard :]
    parts = jnp.pad(parts, ((0, 7), (0, width - 256)))
    keep = jnp.where(first, summed[:shard], summed[shard:])
    back = swap(jnp.concatenate([jnp.where(first, summed[shard:], summed[:shard]), parts], axis=0))
    parts = (parts[0] + back[shard]) * (LN2 / (2.0 * pairs))
    return (
        parts[0],
        jnp.where(first, keep, back[:shard]),
        jnp.where(first, back[:shard], keep),
        parts[128] / logit_scale,
    )


def solution(mesh):
    in_specs = (P(("row", "col"), None), P(("col", "row"), None), P())
    out_specs = (P(), P(("row", "col"), None), P(("col", "row"), None), P())
    return jax.shard_map(
        on_device, mesh=mesh, in_specs=in_specs, out_specs=out_specs, check_vma=False
    )
```

```python
import functools
import itertools

import jax
import jax.numpy as jnp
import numpy as np
from jax import lax
from jax.experimental import pallas as pl
from jax.experimental.pallas import tpu as pltpu
from jax.sharding import PartitionSpec as P

LOG2E = 1.4426950408889634
LN2 = 0.6931471805599453
AXES = ("row", "col")
ROWS = 256
VMEM = 24 * 1024 * 1024
GRAD_VMEM = 63_400_000
SPARE = 3328
EXTRA = 16
PAIR = 2


def linear(x, y, z, core):
    return (((x % 2) * 2 + core) * 4 + z) * 8 + (x // 2) * 4 + y


def devices():
    return itertools.product(range(4), range(4), range(4), range(2))


def partner_perm():
    return [(linear(x, y, z, c), linear(x, y, z, 1 - c)) for x, y, z, c in devices()]


PIECES = ((0, 0), (1, 0), (-1, 0), (0, 1), (2, 0), (-1, 1), (1, 1), (2, 1))


def moved(x, y, z, core, steps, pair):
    if core == 0:
        return (3 - x if pair else x, (y + steps) % 4, z, core)
    return (x ^ 1 if pair else x, y, (z + steps) % 4, core)


def ring_perm(steps, pair):
    return [(linear(*d), linear(*moved(*d, steps, pair))) for d in devices()]


def group_of(x, y, z, core):
    return sorted(linear(*moved(x, y, z, core, steps, pair)) for steps, pair in PIECES)


def groups():
    return sorted(set(tuple(group_of(*d)) for d in devices()))


def block_ids(x, y, z, core):
    out = []
    for steps, pair in PIECES:
        member = linear(*moved(x, y, z, core, steps, pair))
        row, col = member // 32, member % 32
        for c in (0, 1):
            at = (row // 2) * 2 + c
            out.append(at * 32 + col if core == 0 else col * 4 + at)
    return out


def tables():
    table = np.full((128, 32), -1, np.int32)
    for d in devices():
        x, y, z, c = d
        own, other = block_ids(x, y, z, c), block_ids(x, y, z, 1 - c)
        for k, block in enumerate(own):
            if block in other:
                table[linear(*d), k] = other.index(block)
        for side in (0, 1):
            e = (x, y, z, c ^ side)
            for k, (steps, pair) in enumerate(PIECES):
                table[linear(*d), 16 + 8 * side + k] = group_of(*e).index(linear(*moved(*e, steps, pair)))
    return table


def to_column(row):
    n = row.shape[1]
    eye = lax.broadcasted_iota(jnp.int32, (n, n), 0) == lax.broadcasted_iota(jnp.int32, (n, n), 1)
    return jnp.sum(jnp.where(eye, jnp.broadcast_to(row, (n, n)), 0.0), axis=1, keepdims=True)


def eye(n):
    return lax.broadcasted_iota(jnp.int32, (n, n), 0) == lax.broadcasted_iota(jnp.int32, (n, n), 1)


def fetch(parts, whole, sems):
    return [
        pltpu.make_async_copy(part, whole.at[pl.ds(k * ROWS, ROWS)], sems.at[k]) for k, part in enumerate(parts)
    ]


def table_place(table_ref, side, piece):
    return pl.multiple_of(table_ref[16 + 8 * side + piece] * ROWS, ROWS)


def tile_stats(scale, rows, other_at, width, scores_ref):
    chunk = 512 if width % 512 == 0 else 256
    peak = total = weighted = None
    for at in range(0, width, chunk):
        scores = scale * lax.dot_general(
            rows, other_at(at, chunk), (((1,), (1,)), ((), ())), preferred_element_type=jnp.float32
        )
        scores_ref[:, at : at + chunk] = scores
        parts = [scores[:, k : k + 128] for k in range(0, chunk, 128)]
        top = functools.reduce(jnp.maximum, parts)
        if peak is not None:
            top = jnp.maximum(top, peak)
        powers = [jnp.exp2(part - top) for part in parts]
        new_total = functools.reduce(jnp.add, powers)
        new_weighted = functools.reduce(jnp.add, [a * b for a, b in zip(powers, parts)])
        if peak is not None:
            shrink = jnp.exp2(peak - top)
            new_total = new_total + total * shrink
            new_weighted = new_weighted + weighted * shrink
        peak, total, weighted = top, new_total, new_weighted
    peak = peak.T
    top = jnp.max(peak, axis=0, keepdims=True)
    shrink = jnp.exp2(peak - top)
    return (
        top,
        jnp.sum(total.T * shrink, axis=0, keepdims=True),
        jnp.sum(weighted.T * shrink, axis=0, keepdims=True),
    )


def put_matched(table_ref, piece, begin, width, scores_ref, line):
    line[3:4, :] = jnp.zeros((1, ROWS), jnp.float32)
    for half in range(ROWS // 128):
        place = table_ref[piece * (ROWS // 128) + half] * 128 - begin

        @pl.when(jnp.logical_and(place >= 0, place < width))
        def _():
            span = slice(half * 128, half * 128 + 128)
            corner = scores_ref[span, pl.ds(pl.multiple_of(place, 128), 128)]
            line[3:4, span] = jnp.sum(jnp.where(eye(128), corner, 0.0), axis=0, keepdims=True)


def score_kernel(old, new, last, table_ref, scale_ref, *refs):
    total = old + new
    if old:
        before_ref, refs = refs[0], refs[2:]
    own_refs, other_refs = refs[:total], refs[total : 2 * total]
    scores_out, stats_ref, own, other, row, column, line, own_sems, other_sems, out_sems = refs[2 * total :]
    load_own, load_other = fetch(own_refs, own, own_sems), fetch(other_refs, other, other_sems)
    for copy in load_own[old:] + load_other + load_own[:old]:
        copy.start()

    def piece_rows(k):
        return pl.ds(k * ROWS if isinstance(k, int) else pl.multiple_of(k * ROWS, ROWS), ROWS)

    def store_old(k):
        return pltpu.make_async_copy(
            column.at[piece_rows(k)],
            scores_out.at[piece_rows(k), pl.ds(old * ROWS, new * ROWS)],
            out_sems.at[k],
        )

    def store_new(k):
        return pltpu.make_async_copy(
            row.at[piece_rows(k)],
            scores_out.at[piece_rows(k + old), pl.ds(0, total * ROWS)],
            out_sems.at[k + old],
        )

    def put(piece, top, power, weighted):
        line[0:1, :] = top
        line[1:2, :] = power
        line[2:3, :] = weighted
        if last:
            columns = pl.ds(table_place(table_ref, 0, piece), ROWS)
            lse, mean = top + jnp.log2(power), weighted / power
            line[4:5, :] += line[3:4, :]
            for member in range(8):
                stats_ref[member, 0:1, columns] = lse
                stats_ref[member, 1:2, columns] = mean
        else:
            stats_ref[:, piece_rows(piece)] = line[0:4, :]

    def part(at, size):
        if new == 1:
            for k in range(at // ROWS, (at + size) // ROWS):
                load_other[k].wait()
        return other[at : at + size, :]

    def new_piece(k):
        target = row.at[piece_rows(k)]
        top, power, weighted = tile_stats(scale_ref[0], own[piece_rows(k + old), :], part, total * ROWS, target)
        store_new(k).start()
        put_matched(table_ref, k + old, 0, total * ROWS, target, line)
        put(k + old, top, power, weighted)

    def old_scores(k):
        stats = tile_stats(
            scale_ref[0],
            own[piece_rows(k), :],
            lambda at, size: other[old * ROWS + at : old * ROWS + at + size, :],
            new * ROWS,
            column.at[piece_rows(k)],
        )
        store_old(k).start()
        return stats

    def old_stats(k, top, power, weighted):
        put_matched(table_ref, k, old * ROWS, new * ROWS, column.at[piece_rows(k)], line)
        earlier = before_ref[:, piece_rows(k)]
        new_top = jnp.maximum(earlier[0:1], top)
        old_shrink, new_shrink = jnp.exp2(earlier[0:1] - new_top), jnp.exp2(top - new_top)
        line[3:4, :] = earlier[3:4] + line[3:4, :]
        put(k, new_top, earlier[1:2] * old_shrink + power * new_shrink, earlier[2:3] * old_shrink + weighted * new_shrink)

    line[4:5, :] = jnp.zeros((1, ROWS), jnp.float32)
    for copy in load_own[old:] + (load_other if new > 1 else []):
        copy.wait()
    if new == 1:
        new_piece(0)
    else:
        pl.loop(0, new)(new_piece)
    for copy in load_own[:old]:
        copy.wait()
    if new == 1:
        found = [old_scores(k) for k in range(old)]
        for k, stats in enumerate(found):
            old_stats(k, *stats)
    elif old:
        pl.loop(0, old)(lambda k: old_stats(k, *old_scores(k)))
    for k in range(old):
        store_old(k).wait()
    if last:
        matched = jnp.broadcast_to(jnp.sum(line[4:5, :], axis=1, keepdims=True), (2, 128))
        for member in range(8):
            stats_ref[member, :, total * ROWS :] = matched
    for k in range(new):
        store_new(k).wait()


def score_call(name, last, table, scale, before, own, other):
    total, width = len(own), own[0].shape[1]
    old = before[0].shape[1] // ROWS if before else 0
    new = total - old
    smem, vmem, anywhere = (pl.BlockSpec(memory_space=s) for s in (pltpu.SMEM, pltpu.VMEM, pl.ANY))
    tiles = new * total + old * new
    return pl.pallas_call(
        functools.partial(score_kernel, old, new, last),
        in_specs=[smem, smem] + ([vmem, anywhere] if before else []) + [anywhere] * (2 * total),
        out_specs=[anywhere, vmem],
        out_shape=[
            jax.ShapeDtypeStruct((8 * ROWS + SPARE, 8 * ROWS), jnp.float32),
            jax.ShapeDtypeStruct((8, 2, total * ROWS + 128) if last else (4, total * ROWS), jnp.float32),
        ],
        scratch_shapes=[
            pltpu.VMEM((total * ROWS, width), jnp.bfloat16),
            pltpu.VMEM((total * ROWS, width), jnp.bfloat16),
            pltpu.VMEM((new * ROWS, total * ROWS), jnp.float32),
            pltpu.VMEM((max(old, 1) * ROWS, new * ROWS), jnp.float32),
            pltpu.VMEM((8, ROWS), jnp.float32),
            pltpu.SemaphoreType.DMA((total,)),
            pltpu.SemaphoreType.DMA((total,)),
            pltpu.SemaphoreType.DMA((total,)),
        ],
        input_output_aliases={3: 0} if before else {},
        compiler_params=pltpu.CompilerParams(vmem_limit_bytes=VMEM),
        cost_estimate=pl.CostEstimate(
            flops=2 * tiles * ROWS * ROWS * width,
            bytes_accessed=4 * tiles * ROWS * ROWS,
            transcendentals=tiles * ROWS * ROWS,
        ),
        name=name,
    )(table, scale, *before, *own, *other)


def join_kernel(shift, stats_ref, out_ref):
    rows = out_ref.shape[1] - 256
    peak = functools.reduce(jnp.maximum, [stats_ref[k, 0:1, :rows] for k in range(8)])
    total = weighted = matched = 0.0
    for k in range(8):
        power = jnp.exp2(stats_ref[k, 0:1, :rows] - peak)
        total = total + power
        weighted = weighted + stats_ref[k, 1:2, :rows] * power
        matched = matched + stats_ref[k, 0:1, rows:]
    lse = peak + jnp.log2(total)
    out_ref[:, :rows] = lse + shift
    for k, value in enumerate((lse, weighted / total)):
        value = jnp.sum(value, axis=1, keepdims=True)
        out_ref[:, rows + 128 * k : rows + 128 * (k + 1)] = jnp.broadcast_to(value, (1, 128)) - matched


def join_call(shift, stats):
    return pl.pallas_call(
        functools.partial(join_kernel, shift),
        out_shape=jax.ShapeDtypeStruct((1, stats.shape[2] + 128), jnp.float32),
        name="join",
    )(stats)


def grad_kernel(pairs, pieces, table_ref, scale_ref, own_lse_ref, other_lse_ref, scores_ref, *refs):
    count = len(pieces)
    other_refs, outs = refs[:8], refs[8 : 8 + count]
    weights, (blocks, own, other, out_sems, other_sem) = refs[8 + count : 8 + count + PAIR], refs[8 + count + PAIR :]
    step = pl.program_id(0)
    m = scores_ref.shape[1]
    load_other = fetch(other_refs, other, other_sem)
    stores = [
        pltpu.make_async_copy(own if q == 0 else blocks.at[k], outs[k], out_sems.at[k])
        for k, q in enumerate(pieces)
    ]

    @pl.when(step == 0)
    def _():
        for copy in load_other:
            copy.start()

    extra = other_lse_ref[:, m : m + 256]
    high = extra.astype(jnp.bfloat16).astype(jnp.float32)
    middle = (extra - high).astype(jnp.bfloat16).astype(jnp.float32)
    row = lax.broadcasted_iota(jnp.int32, (EXTRA, 256), 0)
    rows = [jnp.broadcast_to(v, (EXTRA, 256)) for v in (high, middle, extra - high - middle)]
    tile = jnp.where(row == 0, rows[0], jnp.where(row == 1, rows[1], jnp.where(row == 2, rows[2], 0.0)))
    ones = eye(128).astype(jnp.float32)

    def weigh(k):
        piece = pieces[k] - PAIR * step
        own_lse = to_column(own_lse_ref[:, pl.ds(table_place(table_ref, 0, piece), ROWS)])
        at_row = (PAIR - 1 - k) * ROWS
        found = [table_ref[piece * (ROWS // 128) + half] for half in range(ROWS // 128)]
        for at in range(0, m, ROWS):
            part = scores_ref[at_row : at_row + ROWS, at : at + ROWS]
            other_lse = other_lse_ref[:, pl.ds(table_place(table_ref, 1, at // ROWS), ROWS)]
            weight = jnp.exp2(part - own_lse) + jnp.exp2(part - other_lse)
            for i in range(0, ROWS, 128):
                for j in range(0, ROWS, 128):
                    taken = jnp.where(found[i // 128] == (at + j) // 128, 1.0 / pairs, 0.0)
                    weights[k][i : i + 128, at + j : at + j + 128] = (
                        weight[i : i + 128, j : j + 128] - ones * taken
                    ).astype(jnp.bfloat16)

    def multiply(k):
        grad = scale_ref[0] * jnp.dot(weights[k][...], other[...], preferred_element_type=jnp.float32)
        slot = PAIR * step + k
        blocks[slot, 0:ROWS, :] = grad.astype(jnp.bfloat16)
        blocks[slot, ROWS:, :] = jnp.zeros((EXTRA, blocks.shape[2]), jnp.bfloat16)
        blocks[slot, ROWS:, 0:256] = tile.astype(jnp.bfloat16)
        if pieces[-1] == 0 and k == PAIR - 1:
            own[...] = grad

    weigh(0)

    @pl.when(step == 0)
    def _():
        for copy in load_other:
            copy.wait()

    multiply(0)
    for k in range(1, PAIR):
        weigh(k)
        multiply(k)
    for at in range(0, count, PAIR):

        @pl.when(step == at // PAIR)
        def _():
            for k in range(at, at + PAIR):
                stores[k].start()

    @pl.when(step == count // PAIR - 1)
    def _():
        for store in stores:
            store.wait()


def grad_call(name, pairs, pieces, table, scale, scores, own_lse, other_lse, other):
    width = other[0].shape[1]
    count = len(pieces)
    m = scores.shape[1]
    smem, vmem, anywhere = (pl.BlockSpec(memory_space=s) for s in (pltpu.SMEM, pltpu.VMEM, pl.ANY))
    sent = jax.ShapeDtypeStruct((ROWS + EXTRA, width), jnp.bfloat16)
    kept = jax.ShapeDtypeStruct((ROWS, width), jnp.float32)
    return pl.pallas_call(
        functools.partial(grad_kernel, pairs, pieces),
        grid=(count // PAIR,),
        in_specs=[
            smem,
            smem,
            vmem,
            vmem,
            pl.BlockSpec((PAIR * ROWS, m), lambda i: (pieces[0] // PAIR - i, 0)),
        ]
        + [anywhere] * 8,
        out_specs=[anywhere] * count,
        out_shape=[kept if q == 0 else sent for q in pieces],
        scratch_shapes=[pltpu.VMEM((ROWS, m), jnp.bfloat16)] * PAIR
        + [
            pltpu.VMEM((count, ROWS + EXTRA, width), jnp.bfloat16),
            pltpu.VMEM((ROWS, width), jnp.float32),
            pltpu.VMEM((m, width), jnp.bfloat16),
            pltpu.SemaphoreType.DMA((count,)),
            pltpu.SemaphoreType.DMA((8,)),
        ],
        compiler_params=pltpu.CompilerParams(vmem_limit_bytes=GRAD_VMEM),
        cost_estimate=pl.CostEstimate(
            flops=2 * count * ROWS * m * width,
            bytes_accessed=4 * count * ROWS * m,
            transcendentals=2 * count * ROWS * m,
        ),
        name=name,
    )(table, scale, own_lse, other_lse, scores, *other)


def on_device(images, texts, logit_scale):
    shard, width = images.shape
    pairs = shard * 128
    me = lax.axis_index(AXES)
    first = lax.rem(lax.axis_index("row"), 2) == 0
    swap = functools.partial(lax.ppermute, axis_name=AXES, perm=partner_perm())
    members = [list(g) for g in groups()]
    table = lax.dynamic_slice(jnp.asarray(tables()), (me, 0), (1, 32)).reshape(-1)
    scale2 = (logit_scale * LOG2E).reshape(1)

    def send(value, steps, pair):
        return lax.ppermute(value, AXES, ring_perm(steps, pair))

    got = swap(jnp.where(first, texts, images))
    mine = jnp.where(first, images, texts)
    chip = jnp.concatenate([jnp.where(first, mine, got), jnp.where(first, got, mine)], axis=0)

    after, before, across = send(chip, -1, 0), send(chip, 1, 0), send(chip, 0, 1)
    own = [chip, after, before, across]
    middle = [send(after, -1, 0), send(across, 1, 0), send(after, 0, 1)]
    other = [swap(v) for v in own]
    scores, stats = score_call("scores_near", False, table, scale2, (), own, other)
    stats, *middle = lax.optimization_barrier((stats, *middle))
    far = send(middle[2], -1, 0)
    own, other = own + middle, other + [swap(v) for v in middle]
    scores, stats = score_call("scores_middle", False, table, scale2, (stats, scores), own, other)
    stats, far = lax.optimization_barrier((stats, far))
    own, other = own + [far], other + [swap(far)]
    scores, stats = score_call("scores_far", True, table, scale2, (stats, scores), own, other)

    spread = lax.all_to_all(stats, AXES, 0, 0, axis_index_groups=members, tiled=True)
    own_lse = join_call(float(np.log2(2.0 * pairs)), spread)
    other_lse = swap(own_lse)

    def grads(name, pieces):
        return grad_call(name, pairs, pieces, table, logit_scale.reshape(1), scores, own_lse, other_lse, other)

    received = [send(v, *PIECES[q]) for q, v in zip((7, 6, 5, 4), grads("grads_far", (7, 6, 5, 4)))]
    *near_grads, kept = grads("grads_near", (3, 2, 1, 0))
    received[:2], near_grads = lax.optimization_barrier((received[:2], near_grads))
    received += [send(v, *PIECES[q]) for q, v in zip((3, 2, 1), near_grads)]
    received = [v.astype(jnp.float32) for v in received]
    summed = functools.reduce(jnp.add, [v[:ROWS] for v in received]) + kept
    parts = functools.reduce(jnp.add, [jnp.sum(v[ROWS : ROWS + 3, 0:256], axis=0, keepdims=True) for v in received])
    parts = parts + other_lse[:, 16 * shard :]
    parts = jnp.pad(parts, ((0, 7), (0, width - 256)))
    keep = jnp.where(first, summed[:shard], summed[shard:])
    back = swap(jnp.concatenate([jnp.where(first, summed[shard:], summed[:shard]), parts], axis=0))
    parts = (parts[0] + back[shard]) * (LN2 / (2.0 * pairs))
    return (
        parts[0],
        jnp.where(first, keep, back[:shard]),
        jnp.where(first, back[:shard], keep),
        parts[128] / logit_scale,
    )


def solution(mesh):
    in_specs = (P(("row", "col"), None), P(("col", "row"), None), P())
    out_specs = (P(), P(("row", "col"), None), P(("col", "row"), None), P())
    return jax.shard_map(
        on_device, mesh=mesh, in_specs=in_specs, out_specs=out_specs, check_vma=False
    )
```
